512 devices in a mesh: grp: 2 (over core), kv: 8 (over z), srv: 32 (over x, y).
Axes of the slice: x: 4, y: 8, z: 8, core: 2. Of those that a mesh axis runs over, the one named last changes fastest.
Arguments:
- queries: bfloat16 [8192, 8, 1024], P('srv', 'kv', 'grp'), may hold values from -120 to 120
- keys: bfloat16 [8192, 8, 128], P('srv', 'kv'), may hold values from -5 to 5
- values: bfloat16 [8192, 8, 128], P('srv', 'kv'), may hold values from -6 to 6
- lengths: int32 [16], replicated, may hold values from 1 to 1024, 8192 in all
- output_projection_weight: bfloat16 [8, 1024, 8192], P('kv', 'grp', 'srv'), may hold values from -0.0625 to 0.0625
Outputs:
- projected: bfloat16 [8192, 8192], P('srv', ('grp', 'kv'))
The draws below stay inside these ranges and needn't reach their ends.
Inputs may be any that keep to these rules, and one draw needn't show every extreme that they name: The 16 lengths sum to 8192; the longest document has exactly 1024 tokens.
All inputs are finite; a program needn't handle non-finite values.
Results may differ from the reference program's by a relative error of at most 0.017.
Values may be sent and summed in bfloat16 or wider, within the bound.
No kernel may reach another device: no remote copies, remote signals or barrier semaphores. Data moves between devices by JAX's collectives and lax.ppermute only.
A program may use at most 64 MiB of HBM per device.

```python
import math
import jax
import jax.numpy as jnp
import numpy as np
from jax import lax

MODEL_WIDTH = 8192
QUERY_HEADS = 64
KEY_VALUE_HEADS = 8
HEAD_WIDTH = 128
TOK_DEV = 256
QUERY_PER_KEY = 8
PACK_TOKENS = 8192
MOST = 1024
DOCS = 16
N_GRP = 2
N_KV = 8
N_SRV = 32


def shared_draw(key):
    base = jax.random.fold_in(key, 1234)
    key_random_seed, query_random_seed = jax.random.split(base, 2)
    key_tensor = jnp.clip(jax.random.normal(key_random_seed, (PACK_TOKENS, KEY_VALUE_HEADS, HEAD_WIDTH), jnp.float32), -5.0, 5.0)
    query_tensor = jnp.clip(jax.random.normal(query_random_seed, (PACK_TOKENS, KEY_VALUE_HEADS, QUERY_PER_KEY * HEAD_WIDTH), jnp.float32), -5.0, 5.0)
    return (query_tensor, key_tensor)


def draw_queries(key, part):
    return shared_draw(key)[0].astype(jnp.bfloat16)


def draw_keys(key, part):
    return shared_draw(key)[1].astype(jnp.bfloat16)


def levels(key, dims, shards, least, high):
    def one(dim, parts):
        heights = jax.random.uniform(jax.random.fold_in(jax.random.fold_in(key, 6), dim), (parts,), jnp.float32, least / len(shards), high / len(shards))
        return jnp.repeat(jnp.exp(heights), dims[dim] // parts).reshape((-1,) + (1,) * (len(dims) - dim - 1))

    factor_of = one(*shards[0])
    for cut in shards[1:]:
        factor_of = factor_of * one(*cut)
    return factor_of


def length_profile(count, total, reach, skew):
    portions = [(1 << 20) // math.isqrt(standing ** skew) + 1 for standing in range(2, count + 1)]
    surplus, given = total - reach - (count - 1), [1] * (count - 1)
    while surplus > 0:
        candidates = [i for i in range(count - 1) if given[i] < reach]
        whole, budget = sum([portions[i] for i in candidates]), surplus
        for i in candidates:
            more = min(reach - given[i], max(1, budget * portions[i] // whole), surplus)
            given[i] = given[i] + more
            surplus = surplus - more
    return np.array([reach] + given)


def uneven_parts(own_key, amount, total, most, slope):
    if amount == 2:
        one = jax.random.randint(own_key, (), max(1, total - most), min(most, total - 1) + 1)
        return jnp.stack([one, total - one])
    tallies = jnp.asarray(length_profile(amount, total, most, slope), jnp.int32)
    couples = (amount - 1) // 2
    giver, receiver = tallies[1:1 + 2 * couples:2], tallies[2:2 + 2 * couples:2]
    margin = jnp.minimum(giver - 1, most - receiver)
    shifted = jax.random.randint(jax.random.fold_in(own_key, 1), (couples,), 0, 1 << 20) % (margin + 1)
    tallies = tallies.at[1:1 + 2 * couples:2].set(giver - shifted).at[2:2 + 2 * couples:2].set(receiver + shifted)
    return tallies[jax.random.permutation(jax.random.fold_in(own_key, 2), amount)]


def normal_values(rng, shape, deviation, bound, cuts=(), held_as=jnp.bfloat16):
    result = deviation * jax.random.normal(rng, shape, jnp.float32)
    if cuts:
        result = result * levels(rng, shape, cuts, -0.22, 0.18)
    return jnp.clip(result, -bound, bound).astype(held_as)


def setup_inputs(seed: int = 0) -> dict:
    key_list = jax.random.split(jax.random.key(seed), 6)
    return {
        "queries": draw_queries(jax.random.fold_in(key_list[5], 71), 0),
        "keys": draw_keys(jax.random.fold_in(key_list[5], 71), 0),
        "values": normal_values(key_list[2], (PACK_TOKENS, KEY_VALUE_HEADS, HEAD_WIDTH), 1.0, 6.0, ((0, 32), (1, 8))),
        "lengths": uneven_parts(key_list[3], DOCS, PACK_TOKENS, MOST, 2).astype(jnp.int32),
        "output_projection_weight": normal_values(key_list[4], (KEY_VALUE_HEADS, QUERY_PER_KEY * HEAD_WIDTH, MODEL_WIDTH), (QUERY_HEADS * HEAD_WIDTH) ** -0.5, 0.0625, ((0, 8), (1, 2), (2, 32))),
    }


def doc_starts(lengths, position):
    starts = jnp.cumsum(lengths) - lengths
    chosen = jnp.where(starts[None, :] <= position[:, None], starts[None, :], 0)
    return lax.optimization_barrier(jnp.max(chosen, axis=1))

def attend_exact(query_block_rows, window_keys, window_values, query_pos, key_pos, lengths):
    token_count = query_block_rows.shape[0]
    split_output = query_block_rows.astype(jnp.float32).reshape(token_count, KEY_VALUE_HEADS, QUERY_PER_KEY, HEAD_WIDTH)
    scores = jnp.einsum('tjhd,wjd->jhtw', split_output, window_keys.astype(jnp.float32)) * (1.0 / math.sqrt(HEAD_WIDTH))
    first_key = doc_starts(lengths, query_pos)
    allowed = (key_pos[None, :] >= first_key[:, None]) & (key_pos[None, :] <= query_pos[:, None])
    scores = jnp.where(allowed[None, None], scores, -jnp.inf)
    peak = lax.optimization_barrier(jnp.max(scores, axis=3, keepdims=True))
    weights = jnp.exp(scores - peak)
    total = lax.optimization_barrier(jnp.sum(weights, axis=3))
    rounded = lax.optimization_barrier(weights.astype(jnp.bfloat16))
    numer = jnp.einsum('jhtw,wjd->tjhd', rounded.astype(jnp.float32), window_values.astype(jnp.float32))
    final_output = numer / jnp.transpose(total, (2, 0, 1))[..., None]
    return final_output.astype(jnp.bfloat16).reshape(token_count, KEY_VALUE_HEADS, QUERY_PER_KEY * HEAD_WIDTH)

def reference(queries, keys, values, lengths, output_projection_weight):
    window = MOST + TOK_DEV
    keys_padded = jnp.pad(keys, ((MOST, 0), (0, 0), (0, 0)))
    values_padded = jnp.pad(values, ((MOST, 0), (0, 0), (0, 0)))

    def one_block(index):
        start = index * TOK_DEV
        query_block_rows = lax.dynamic_slice_in_dim(queries, start, TOK_DEV, 0)
        window_keys = lax.dynamic_slice_in_dim(keys_padded, start, window, 0)
        window_values = lax.dynamic_slice_in_dim(values_padded, start, window, 0)
        query_pos = start + jnp.arange(TOK_DEV, dtype=jnp.int32)
        key_pos = start - MOST + jnp.arange(window, dtype=jnp.int32)
        return attend_exact(query_block_rows, window_keys, window_values, query_pos, key_pos, lengths)
    block_list = lax.map(one_block, jnp.arange(N_SRV, dtype=jnp.int32))
    attention_output = block_list.reshape(PACK_TOKENS, KEY_VALUE_HEADS, QUERY_PER_KEY * HEAD_WIDTH)
    heads_per_group = KEY_VALUE_HEADS // N_KV
    half_width = QUERY_PER_KEY * HEAD_WIDTH // N_GRP
    attended_split = attention_output.reshape(PACK_TOKENS, N_KV, heads_per_group, N_GRP, half_width)
    weight_split = output_projection_weight.reshape(N_KV, heads_per_group, N_GRP, half_width, MODEL_WIDTH)
    summed = jnp.zeros((PACK_TOKENS, MODEL_WIDTH), jnp.float32)
    for half_index in range(N_GRP):
        for group_index in range(N_KV):
            left = attended_split[:, group_index, :, half_index, :].reshape(PACK_TOKENS, heads_per_group * half_width)
            right = weight_split[group_index, :, half_index].reshape(heads_per_group * half_width, MODEL_WIDTH)
            partial_sum = jnp.dot(left, right, preferred_element_type=jnp.float32).astype(jnp.bfloat16)
            partial_sum = lax.optimization_barrier(partial_sum)
            summed = summed + partial_sum.astype(jnp.float32)
    return summed.astype(jnp.bfloat16)
```

```python
import functools
import math

import jax
import jax.numpy as jnp
from jax import lax
from jax.experimental import pallas as pl
from jax.experimental.pallas import tpu as pltpu
from jax.sharding import PartitionSpec as P

REACH = 4
ALL = ("grp", "kv", "srv")


def doc_starts(lengths, position):
    count = lengths.shape[0]
    before = jnp.arange(count)[None, :] < jnp.arange(count)[:, None]
    starts = jnp.sum(jnp.where(before, lengths[None, :], 0), axis=1)
    chosen = jnp.where(starts[None, :] <= position[:, None], starts[None, :], 0)
    return jnp.max(chosen, axis=1)


def attend(queries, window_keys, window_values, query_pos, key_pos, lengths):
    token_count = queries.shape[0]
    head_size = window_keys.shape[1]
    heads = queries.shape[1] // head_size
    split = queries.reshape(token_count, heads, head_size)
    scores = jnp.einsum("thd,wd->htw", split, window_keys, preferred_element_type=jnp.float32)
    scores = scores * (1.0 / math.sqrt(head_size))
    first_key = doc_starts(lengths, query_pos)
    allowed = (key_pos[None, :] >= first_key[:, None]) & (key_pos[None, :] <= query_pos[:, None])
    scores = jnp.where(allowed[None], scores, -jnp.inf)
    peak = jnp.max(scores, axis=2, keepdims=True)
    weights = jnp.exp(scores - peak)
    total = jnp.sum(weights, axis=2)
    numer = jnp.einsum(
        "htw,wd->thd", weights.astype(jnp.bfloat16), window_values, preferred_element_type=jnp.float32
    )
    result = numer / jnp.transpose(total, (1, 0))[..., None]
    return result.astype(jnp.bfloat16).reshape(token_count, heads * head_size)


def window_of(stacked, core, n_srv):
    def fetch(near):
        route = []
        for c in range(2):
            distance = near + 2 * c
            route += [(c * n_srv + i - distance, c * n_srv + i) for i in range(distance, n_srv)]
        return lax.ppermute(stacked, ("grp", "srv"), route)

    mine = jnp.concatenate([fetch(1), fetch(2)], axis=1)
    other = lax.ppermute(mine, "grp", [(0, 1), (1, 0)])
    window = jnp.concatenate([mine, other, stacked], axis=1)
    behind = jnp.stack([1 + 2 * core, 2 + 2 * core, 3 - 2 * core, 4 - 2 * core, 0 * core])
    return window, behind


def product_kernel(steps, left_ref, right_ref, out_ref, total_ref):
    step = pl.program_id(0)

    @pl.when(step == 0)
    def _():
        total_ref[...] = jnp.zeros_like(total_ref)

    left = left_ref[0]
    width = right_ref.shape[3]
    for half in range(right_ref.shape[0]):
        total_ref[:, half * width : (half + 1) * width] += jnp.dot(
            left, right_ref[half, 0], preferred_element_type=jnp.float32
        )

    @pl.when(step == steps - 1)
    def _():
        out_ref[...] = total_ref[...].astype(out_ref.dtype)


def product(left, right):
    steps, tokens, depth = left.shape
    halves, _, _, width = right.shape
    return pl.pallas_call(
        functools.partial(product_kernel, steps),
        grid=(steps,),
        out_shape=jax.ShapeDtypeStruct((tokens, halves * width), jnp.bfloat16),
        in_specs=[
            pl.BlockSpec((1, tokens, depth), lambda s: (s, 0, 0)),
            pl.BlockSpec((halves, 1, depth, width), lambda s: (0, s, 0, 0)),
        ],
        out_specs=pl.BlockSpec((tokens, halves * width), lambda s: (0, 0)),
        scratch_shapes=[pltpu.VMEM((tokens, halves * width), jnp.float32)],
        compiler_params=pltpu.CompilerParams(vmem_limit_bytes=58 * 2**20),
        cost_estimate=pl.CostEstimate(
            flops=2 * steps * tokens * depth * halves * width,
            bytes_accessed=2 * (left.size + right.size + tokens * halves * width),
            transcendentals=0,
        ),
    )(left, right)


def solution(mesh):
    n_grp, n_kv, n_srv = mesh.shape["grp"], mesh.shape["kv"], mesh.shape["srv"]
    blocks = n_grp * n_kv
    halves = n_srv // blocks

    to_owner = []
    for c in range(n_grp):
        for z in range(n_kv):
            for s in range(n_srv):
                owner = s // halves
                place = (s % halves) * blocks + c * n_kv + z
                to_owner.append(((c * n_kv + z) * n_srv + s, owner * n_srv + place))

    def on_device(queries, keys, values, lengths, weight):
        tokens = queries.shape[0]
        core = lax.axis_index("grp")
        shard = lax.axis_index("srv")
        weight = lax.ppermute(weight[0], ALL, to_owner)
        columns = lax.all_gather(weight, "srv", axis=0, tiled=True)
        columns = columns.reshape(halves, blocks, weight.shape[0], weight.shape[1])

        window, behind = window_of(jnp.stack([keys[:, 0], values[:, 0]]), core, n_srv)
        query_pos = shard * tokens + jnp.arange(tokens, dtype=jnp.int32)
        key_pos = ((shard - behind) * tokens)[:, None] + jnp.arange(tokens, dtype=jnp.int32)[None, :]
        heads = attend(queries[:, 0], window[0], window[1], query_pos, key_pos.reshape(-1), lengths)
        along = lax.all_to_all(jnp.broadcast_to(heads, (n_kv,) + heads.shape), "kv", 0, 0)
        both = lax.all_to_all(jnp.broadcast_to(along, (n_grp,) + along.shape), "grp", 0, 0)
        return product(both.reshape(blocks, tokens, heads.shape[1]), columns)

    placed = (P("srv", "kv", "grp"), P("srv", "kv", None), P("srv", "kv", None), P(), P("kv", "grp", "srv"))
    return jax.shard_map(
        on_device, mesh=mesh, in_specs=placed, out_specs=P("srv", ("grp", "kv")), check_vma=False
    )
```

```python
import math

import jax
import jax.numpy as jnp
from jax import lax
from jax.experimental import pallas as pl
from jax.experimental.pallas import tpu as pltpu
from jax.sharding import PartitionSpec as P

REACH = 4
ALL = ("grp", "kv", "sx", "sy")
SX = 4


def doc_starts(lengths, position):
    count = lengths.shape[0]
    before = jnp.arange(count)[None, :] < jnp.arange(count)[:, None]
    starts = jnp.sum(jnp.where(before, lengths[None, :], 0), axis=1)
    chosen = jnp.where(starts[None, :] <= position[:, None], starts[None, :], 0)
    return jnp.max(chosen, axis=1)


def attend(queries, window_keys, window_values, query_pos, key_pos, lengths):
    token_count = queries.shape[0]
    head_size = window_keys.shape[1]
    heads = queries.shape[1] // head_size
    split = queries.reshape(token_count, heads, head_size)
    scores = jnp.einsum("thd,wd->htw", split, window_keys, preferred_element_type=jnp.float32)
    scores = scores * (1.0 / math.sqrt(head_size))
    first_key = doc_starts(lengths, query_pos)
    allowed = (key_pos[None, :] >= first_key[:, None]) & (key_pos[None, :] <= query_pos[:, None])
    scores = jnp.where(allowed[None], scores, -jnp.inf)
    peak = jnp.max(scores, axis=2, keepdims=True)
    weights = jnp.exp(scores - peak)
    total = jnp.sum(weights, axis=2)
    numer = jnp.einsum(
        "htw,wd->thd", weights.astype(jnp.bfloat16), window_values, preferred_element_type=jnp.float32
    )
    result = numer / jnp.transpose(total, (1, 0))[..., None]
    return result.astype(jnp.bfloat16).reshape(token_count, heads * head_size)


def window_of(stacked, core, n_srv):
    def fetch(near):
        route = []
        for c in range(2):
            distance = near + 2 * c
            route += [(c * n_srv + i - distance, c * n_srv + i) for i in range(distance, n_srv)]
        return lax.ppermute(stacked, ("grp", "sx", "sy"), route)

    mine = jnp.concatenate([fetch(1), fetch(2)], axis=1)
    other = lax.ppermute(mine, "grp", [(0, 1), (1, 0)])
    window = jnp.concatenate([mine, other, stacked], axis=1)
    behind = jnp.stack([1 + 2 * core, 2 + 2 * core, 3 - 2 * core, 4 - 2 * core, 0 * core])
    return window, behind


def product_kernel(left_ref, right_ref, out_ref):
    right = jnp.concatenate([right_ref[0], right_ref[1]], axis=1)
    for block in range(left_ref.shape[0]):
        out_ref[0, block] = jnp.dot(
            left_ref[block], right, preferred_element_type=jnp.float32
        ).astype(out_ref.dtype)


def product(left, right):
    blocks, tokens, depth = left.shape
    pieces, _, width = right.shape
    tiles = pieces // 2
    return pl.pallas_call(
        product_kernel,
        grid=(tiles,),
        out_shape=jax.ShapeDtypeStruct((tiles, blocks, tokens, 2 * width), jnp.bfloat16),
        in_specs=[
            pl.BlockSpec((blocks, tokens, depth), lambda j: (0, 0, 0)),
            pl.BlockSpec((2, depth, width), lambda j: (j, 0, 0)),
        ],
        out_specs=pl.BlockSpec((1, blocks, tokens, 2 * width), lambda j: (j, 0, 0, 0)),
        compiler_params=pltpu.CompilerParams(vmem_limit_bytes=58 * 2**20),
        cost_estimate=pl.CostEstimate(
            flops=2 * blocks * tokens * depth * pieces * width,
            bytes_accessed=2 * (left.size + right.size + blocks * tokens * pieces * width),
            transcendentals=0,
        ),
    )(left, right)


def solution(mesh):
    n_grp, n_kv, n_srv = mesh.shape["grp"], mesh.shape["kv"], mesh.shape["srv"]
    sy = n_srv // SX
    fine = jax.sharding.Mesh(mesh.devices.reshape(n_grp, n_kv, SX, sy), ALL)
    tiles = n_grp * n_kv // SX

    to_owner = []
    for c in range(n_grp):
        for z in range(n_kv):
            for x in range(SX):
                j, to_x = divmod(z * n_grp + c, SX)
                owner = x * tiles + j
                for y in range(sy):
                    to_owner.append((((c * n_kv + z) * SX + x) * sy + y, (owner * SX + to_x) * sy + y))

    def on_device(queries, keys, values, lengths, weight):
        tokens = queries.shape[0]
        core = lax.axis_index("grp")
        shard = lax.axis_index("sx") * sy + lax.axis_index("sy")
        columns = lax.all_gather(weight[0], "sy", axis=0, tiled=True)
        columns = columns.reshape(sy, weight.shape[1], weight.shape[2])

        window, behind = window_of(jnp.stack([keys[:, 0], values[:, 0]]), core, n_srv)
        query_pos = shard * tokens + jnp.arange(tokens, dtype=jnp.int32)
        key_pos = ((shard - behind) * tokens)[:, None] + jnp.arange(tokens, dtype=jnp.int32)[None, :]
        heads = attend(queries[:, 0], window[0], window[1], query_pos, key_pos.reshape(-1), lengths)
        along = lax.all_to_all(jnp.broadcast_to(heads, (SX,) + heads.shape), "sx", 0, 0)
        partial = product(along, columns)
        partial = partial.reshape(n_kv * n_grp * tokens, partial.shape[3])
        summed = lax.psum_scatter(partial, "kv", scatter_dimension=0, tiled=True)
        summed = lax.all_to_all(summed.reshape(n_grp, tokens, summed.shape[1]), "grp", 0, 0)
        tile = jnp.sum(summed.astype(jnp.float32), axis=0).astype(jnp.bfloat16)
        return lax.ppermute(tile, ALL, to_owner)

    q = P(("sx", "sy"), "kv", "grp")
    k = P(("sx", "sy"), "kv", None)
    placed = (q, k, k, P(), P("kv", "grp", ("sx", "sy")))
    return jax.shard_map(
        on_device, mesh=fine, in_specs=placed, out_specs=P(("sx", "sy"), ("grp", "kv")), check_vma=False
    )
```

```python
import math

import jax
import jax.numpy as jnp
from jax import lax
from jax.experimental import pallas as pl
from jax.experimental.pallas import tpu as pltpu
from jax.sharding import PartitionSpec as P

REACH = 4
ALL = ("grp", "zh", "zl", "sx", "sy")
SX = 4
ZL = 2


def doc_starts(lengths, position):
    count = lengths.shape[0]
    before = jnp.arange(count)[None, :] < jnp.arange(count)[:, None]
    starts = jnp.sum(jnp.where(before, lengths[None, :], 0), axis=1)
    chosen = jnp.where(starts[None, :] <= position[:, None], starts[None, :], 0)
    return jnp.max(chosen, axis=1)


def attend(queries, window_keys, window_values, query_pos, key_pos, lengths):
    token_count = queries.shape[0]
    head_size = window_keys.shape[1]
    heads = queries.shape[1] // head_size
    split = queries.reshape(token_count, heads, head_size)
    scores = jnp.einsum("thd,wd->htw", split, window_keys, preferred_element_type=jnp.float32)
    scores = scores * (1.0 / math.sqrt(head_size))
    first_key = doc_starts(lengths, query_pos)
    allowed = (key_pos[None, :] >= first_key[:, None]) & (key_pos[None, :] <= query_pos[:, None])
    scores = jnp.where(allowed[None], scores, -jnp.inf)
    peak = jnp.max(scores, axis=2, keepdims=True)
    weights = jnp.exp(scores - peak)
    total = jnp.sum(weights, axis=2)
    numer = jnp.einsum(
        "htw,wd->thd", weights.astype(jnp.bfloat16), window_values, preferred_element_type=jnp.float32
    )
    result = numer / jnp.transpose(total, (1, 0))[..., None]
    return result.astype(jnp.bfloat16).reshape(token_count, heads * head_size)


def window_of(stacked, core, n_srv):
    def fetch(near):
        route = []
        for c in range(2):
            distance = near + 2 * c
            route += [(c * n_srv + i - distance, c * n_srv + i) for i in range(distance, n_srv)]
        return lax.ppermute(stacked, ("grp", "sx", "sy"), route)

    mine = jnp.concatenate([fetch(1), fetch(2)], axis=1)
    other = lax.ppermute(mine, "grp", [(0, 1), (1, 0)])
    window = jnp.concatenate([mine, other, stacked], axis=1)
    behind = jnp.stack([1 + 2 * core, 2 + 2 * core, 3 - 2 * core, 4 - 2 * core, 0 * core])
    return window, behind


def product_kernel(left_ref, right_ref, out_ref):
    cores, pairs = left_ref.shape[:2]
    left = jnp.concatenate([left_ref[c, z, 0] for z in range(pairs) for c in range(cores)], axis=1)
    halves, parts, depth, width = right_ref.shape
    for half in range(halves):
        out_ref[0, :, half * width : (half + 1) * width] = jnp.dot(
            left, right_ref[half].reshape(parts * depth, width), preferred_element_type=jnp.float32
        ).astype(out_ref.dtype)


def product(left, right):
    cores, pairs, blocks, tokens, depth = left.shape
    halves, parts, _, width = right.shape
    return pl.pallas_call(
        product_kernel,
        grid=(blocks,),
        out_shape=jax.ShapeDtypeStruct((blocks, tokens, halves * width), jnp.bfloat16),
        in_specs=[
            pl.BlockSpec((cores, pairs, 1, tokens, depth), lambda i: (0, 0, i, 0, 0)),
            pl.BlockSpec((halves, parts, depth, width), lambda i: (0, 0, 0, 0)),
        ],
        out_specs=pl.BlockSpec((1, tokens, halves * width), lambda i: (i, 0, 0)),
        compiler_params=pltpu.CompilerParams(vmem_limit_bytes=58 * 2**20),
        cost_estimate=pl.CostEstimate(
            flops=2 * left.size * halves * width,
            bytes_accessed=2 * (left.size + right.size + blocks * tokens * halves * width),
            transcendentals=0,
        ),
    )(left, right)


def solution(mesh):
    n_grp, n_kv, n_srv = mesh.shape["grp"], mesh.shape["kv"], mesh.shape["srv"]
    sy, zh = n_srv // SX, n_kv // ZL
    sizes = (n_grp, zh, ZL, SX, sy)
    fine = jax.sharding.Mesh(mesh.devices.reshape(sizes), ALL)

    def index(*place):
        total = 0
        for at, size in zip(place, sizes):
            total = total * size + at
        return total

    to_ring, to_owner = [], []
    for c in range(n_grp):
        for hi in range(zh):
            for lo in range(ZL):
                for x in range(SX):
                    for y in range(sy):
                        a, z = divmod((x * sy + y) // 2, n_kv)
                        g, w = divmod(z // 2, ZL)
                        ring = index(g, hi, w, 2 * a + z % 2, (y % 2) * 4 + lo * 2 + c)
                        to_ring.append((index(c, hi, lo, x, y), ring))
                        z = 2 * (c * ZL + lo) + x % 2
                        owner = index(x // 2, z // ZL, z % ZL, hi, y)
                        to_owner.append((index(c, hi, lo, x, y), owner))

    def on_device(queries, keys, values, lengths, weight):
        tokens = queries.shape[0]
        core = lax.axis_index("grp")
        shard = lax.axis_index("sx") * sy + lax.axis_index("sy")
        weight = lax.ppermute(weight[0], ALL, to_ring)
        columns = lax.all_gather(weight, "sy", axis=0, tiled=True)
        columns = columns.reshape(2, ZL * n_grp, weight.shape[0], weight.shape[1])

        window, behind = window_of(jnp.stack([keys[:, 0], values[:, 0]]), core, n_srv)
        query_pos = shard * tokens + jnp.arange(tokens, dtype=jnp.int32)
        key_pos = ((shard - behind) * tokens)[:, None] + jnp.arange(tokens, dtype=jnp.int32)[None, :]
        heads = attend(queries[:, 0], window[0], window[1], query_pos, key_pos.reshape(-1), lengths)
        along = lax.all_to_all(jnp.broadcast_to(heads, (ZL * SX,) + heads.shape), ("zl", "sx"), 0, 0)
        both = lax.all_to_all(jnp.broadcast_to(along, (n_grp,) + along.shape), "grp", 0, 0)
        partial = product(both.reshape((n_grp, ZL, SX) + heads.shape), columns)
        parts = lax.all_to_all(partial, "zh", 0, 0)
        tile = jnp.sum(parts.astype(jnp.float32), axis=0).astype(jnp.bfloat16)
        return lax.ppermute(tile, ALL, to_owner)

    q = P(("sx", "sy"), ("zh", "zl"), "grp")
    k = P(("sx", "sy"), ("zh", "zl"), None)
    placed = (q, k, k, P(), P(("zh", "zl"), "grp", ("sx", "sy")))
    return jax.shard_map(
        on_device, mesh=fine, in_specs=placed, out_specs=P(("sx", "sy"), ("grp", "zh", "zl")), check_vma=False
    )
```

```python
import math

import jax
import jax.numpy as jnp
from jax import lax
from jax.experimental import pallas as pl
from jax.experimental.pallas import tpu as pltpu
from jax.sharding import PartitionSpec as P

REACH = 4
ALL = ("grp", "zh", "zl", "sx", "sy")
SX = 4
ZL = 2


def doc_starts(lengths, position):
    count = lengths.shape[0]
    before = jnp.arange(count)[None, :] < jnp.arange(count)[:, None]
    starts = jnp.sum(jnp.where(before, lengths[None, :], 0), axis=1)
    chosen = jnp.where(starts[None, :] <= position[:, None], starts[None, :], 0)
    return jnp.max(chosen, axis=1)


def attend(queries, window_keys, window_values, query_pos, key_pos, lengths):
    token_count = queries.shape[0]
    head_size = window_keys.shape[1]
    heads = queries.shape[1] // head_size
    split = queries.reshape(token_count, heads, head_size)
    scores = jnp.einsum("thd,wd->htw", split, window_keys, preferred_element_type=jnp.float32)
    scores = scores * (1.0 / math.sqrt(head_size))
    first_key = doc_starts(lengths, query_pos)
    allowed = (key_pos[None, :] >= first_key[:, None]) & (key_pos[None, :] <= query_pos[:, None])
    scores = jnp.where(allowed[None], scores, -jnp.inf)
    peak = jnp.max(scores, axis=2, keepdims=True)
    weights = jnp.exp(scores - peak)
    total = jnp.sum(weights, axis=2)
    numer = jnp.einsum(
        "htw,wd->thd", weights.astype(jnp.bfloat16), window_values, preferred_element_type=jnp.float32
    )
    result = numer / jnp.transpose(total, (1, 0))[..., None]
    return result.astype(jnp.bfloat16).reshape(token_count, heads * head_size)


def fetch_behind(stacked, near, n_srv):
    route = []
    for c in range(2):
        distance = near + 2 * c
        route += [(c * n_srv + i - distance, c * n_srv + i) for i in range(distance, n_srv)]
    return lax.ppermute(stacked, ("grp", "sx", "sy"), route)


def product_kernel(own_ref, other_ref, right_ref, out_ref):
    left = jnp.concatenate(
        [ref[z, 0] for z in range(own_ref.shape[0]) for ref in (own_ref, other_ref)], axis=1
    )
    halves, parts, depth, width = right_ref.shape
    for half in range(halves):
        out_ref[0, :, half * width : (half + 1) * width] = jnp.dot(
            left, right_ref[half].reshape(parts * depth, width), preferred_element_type=jnp.float32
        ).astype(out_ref.dtype)


def product(own, other, right):
    pairs, blocks, tokens, depth = own.shape
    halves, parts, _, width = right.shape
    heads = pl.BlockSpec((pairs, 1, tokens, depth), lambda i: (0, i, 0, 0))
    return pl.pallas_call(
        product_kernel,
        grid=(blocks,),
        out_shape=jax.ShapeDtypeStruct((blocks, tokens, halves * width), jnp.bfloat16),
        in_specs=[heads, heads, pl.BlockSpec((halves, parts, depth, width), lambda i: (0, 0, 0, 0))],
        out_specs=pl.BlockSpec((1, tokens, halves * width), lambda i: (i, 0, 0)),
        compiler_params=pltpu.CompilerParams(vmem_limit_bytes=58 * 2**20),
        cost_estimate=pl.CostEstimate(
            flops=4 * own.size * halves * width,
            bytes_accessed=2 * (2 * own.size + right.size + blocks * tokens * halves * width),
            transcendentals=0,
        ),
    )(own, other, right)


def solution(mesh):
    n_grp, n_kv, n_srv = mesh.shape["grp"], mesh.shape["kv"], mesh.shape["srv"]
    sy, zh = n_srv // SX, n_kv // ZL
    sizes = (n_grp, zh, ZL, SX, sy)
    fine = jax.sharding.Mesh(mesh.devices.reshape(sizes), ALL)

    def index(*place):
        total = 0
        for at, size in zip(place, sizes):
            total = total * size + at
        return total

    to_ring, to_owner = [], []
    for c in range(n_grp):
        for hi in range(zh):
            for lo in range(ZL):
                for x in range(SX):
                    for y in range(sy):
                        a, z = divmod((x * sy + y) // 2, n_kv)
                        g, w = divmod(z // 2, ZL)
                        ring = index(g, hi, w, 2 * a + z % 2, (y % 2) * 4 + lo * 2 + (c ^ g))
                        to_ring.append((index(c, hi, lo, x, y), ring))
                        z = 2 * (c * ZL + lo) + x % 2
                        owner = index(x // 2, z // ZL, z % ZL, hi, y)
                        to_owner.append((index(c, hi, lo, x, y), owner))

    def on_device(queries, keys, values, lengths, weight):
        tokens = queries.shape[0]
        core = lax.axis_index("grp")
        shard = lax.axis_index("sx") * sy + lax.axis_index("sy")
        stacked = jnp.stack([keys[:, 0], values[:, 0]])
        mine = jnp.concatenate([fetch_behind(stacked, 1, n_srv), fetch_behind(stacked, 2, n_srv)], axis=1)
        weight = lax.ppermute(weight[0], ALL, to_ring)
        mine, weight = lax.optimization_barrier((mine, weight))
        columns = lax.all_gather(weight, "sy", axis=0, tiled=True)
        columns = columns.reshape(2, ZL * n_grp, weight.shape[0], weight.shape[1])

        def gather_heads(queries, stacked, mine, lengths):
            window = jnp.concatenate([mine, lax.ppermute(mine, "grp", [(0, 1), (1, 0)]), stacked], axis=1)
            behind = jnp.stack([1 + 2 * core, 2 + 2 * core, 3 - 2 * core, 4 - 2 * core, 0 * core])
            query_pos = shard * tokens + jnp.arange(tokens, dtype=jnp.int32)
            key_pos = ((shard - behind) * tokens)[:, None] + jnp.arange(tokens, dtype=jnp.int32)[None, :]
            heads = attend(queries, window[0], window[1], query_pos, key_pos.reshape(-1), lengths)
            along = lax.all_to_all(jnp.broadcast_to(heads, (ZL * SX,) + heads.shape), ("zl", "sx"), 0, 0)
            own = along.reshape((ZL, SX) + heads.shape)
            return own, lax.ppermute(own, "grp", [(0, 1), (1, 0)])

        def nothing(queries, stacked, mine, lengths):
            empty = jnp.zeros((ZL, SX) + queries.shape, queries.dtype)
            return empty, empty

        own, other = lax.cond(lengths[0] > 0, gather_heads, nothing, queries[:, 0], stacked, mine, lengths)
        partial = product(own, other, columns)
        parts = lax.all_to_all(partial, "zh", 0, 0)
        tile = jnp.sum(parts.astype(jnp.float32), axis=0).astype(jnp.bfloat16)
        return lax.ppermute(tile, ALL, to_owner)

    q = P(("sx", "sy"), ("zh", "zl"), "grp")
    k = P(("sx", "sy"), ("zh", "zl"), None)
    placed = (q, k, k, P(), P(("zh", "zl"), "grp", ("sx", "sy")))
    return jax.shard_map(
        on_device, mesh=fine, in_specs=placed, out_specs=P(("sx", "sy"), ("grp", "zh", "zl")), check_vma=False
    )
```

```python
import math

import jax
import jax.numpy as jnp
from jax import lax
from jax.experimental import pallas as pl
from jax.experimental.pallas import tpu as pltpu
from jax.sharding import PartitionSpec as P

REACH = 4
ALL = ("grp", "zh", "zl", "sx", "sy")
SX = 4
ZL = 2


def doc_starts(lengths, position):
    count = lengths.shape[0]
    before = jnp.arange(count)[None, :] < jnp.arange(count)[:, None]
    starts = jnp.sum(jnp.where(before, lengths[None, :], 0), axis=1)
    chosen = jnp.where(starts[None, :] <= position[:, None], starts[None, :], 0)
    return jnp.max(chosen, axis=1)


def attend(queries, window_keys, window_values, query_pos, key_pos, lengths):
    token_count = queries.shape[0]
    head_size = window_keys.shape[1]
    heads = queries.shape[1] // head_size
    split = queries.reshape(token_count, heads, head_size)
    scores = jnp.einsum("thd,wd->htw", split, window_keys, preferred_element_type=jnp.float32)
    scores = scores * (1.0 / math.sqrt(head_size))
    first_key = doc_starts(lengths, query_pos)
    allowed = (key_pos[None, :] >= first_key[:, None]) & (key_pos[None, :] <= query_pos[:, None])
    scores = jnp.where(allowed[None], scores, -jnp.inf)
    peak = jnp.max(scores, axis=2, keepdims=True)
    weights = jnp.exp(scores - peak)
    total = jnp.sum(weights, axis=2)
    numer = jnp.einsum(
        "htw,wd->thd", weights.astype(jnp.bfloat16), window_values, preferred_element_type=jnp.float32
    )
    result = numer / jnp.transpose(total, (1, 0))[..., None]
    return result.astype(jnp.bfloat16).reshape(token_count, heads * head_size)


def fetch_behind(stacked, near, n_srv):
    route = []
    for c in range(2):
        distance = near + 2 * c
        route += [(c * n_srv + i - distance, c * n_srv + i) for i in range(distance, n_srv)]
    return lax.ppermute(stacked, ("grp", "sx", "sy"), route)


def product_kernel(turn_ref, *refs):
    *left_refs, right_ref, out_ref = refs
    left = jnp.concatenate([ref[0] for ref in left_refs], axis=1)
    _, parts, depth, width = right_ref.shape
    right = right_ref[0].reshape(parts * depth, width)
    out_ref[...] = jnp.dot(left, right, preferred_element_type=jnp.float32).astype(out_ref.dtype)


def product(turn, lefts, right):
    _, tokens, depth = lefts[0].shape
    halves, parts, _, width = right.shape
    heads = pl.BlockSpec((1, tokens, depth), lambda h, turn: (turn[0], 0, 0))
    grid_spec = pltpu.PrefetchScalarGridSpec(
        num_scalar_prefetch=1,
        grid=(halves,),
        in_specs=[heads] * parts + [pl.BlockSpec((1, parts, depth, width), lambda h, turn: (h, 0, 0, 0))],
        out_specs=pl.BlockSpec((tokens, width), lambda h, turn: (0, h)),
    )
    return pl.pallas_call(
        product_kernel,
        grid_spec=grid_spec,
        out_shape=jax.ShapeDtypeStruct((tokens, halves * width), jnp.bfloat16),
        compiler_params=pltpu.CompilerParams(vmem_limit_bytes=58 * 2**20),
        cost_estimate=pl.CostEstimate(
            flops=2 * tokens * right.size,
            bytes_accessed=2 * (parts * tokens * depth + right.size + tokens * halves * width),
            transcendentals=0,
        ),
    )(turn.reshape(1), *lefts, right)


def solution(mesh):
    n_grp, n_kv, n_srv = mesh.shape["grp"], mesh.shape["kv"], mesh.shape["srv"]
    sy, zh = n_srv // SX, n_kv // ZL
    sizes = (n_grp, zh, ZL, SX, sy)
    fine = jax.sharding.Mesh(mesh.devices.reshape(sizes), ALL)

    def index(*place):
        total = 0
        for at, size in zip(place, sizes):
            total = total * size + at
        return total

    to_ring, to_owner = [], [[] for _ in range(SX)]
    for c in range(n_grp):
        for hi in range(zh):
            for lo in range(ZL):
                for x in range(SX):
                    for y in range(sy):
                        a, z = divmod((x * sy + y) // 2, n_kv)
                        g, w = divmod(z // 2, ZL)
                        ring = index(g, hi, w, 2 * a + z % 2, (y % 2) * 4 + (lo ^ w) * 2 + (c ^ g))
                        to_ring.append((index(c, hi, lo, x, y), ring))
                        z = 2 * (c * ZL + lo) + x % 2
                        for t in range(SX):
                            owner = index(x // 2, z // ZL, z % ZL, (hi + t) % SX, y)
                            to_owner[t].append((index(c, hi, lo, x, y), owner))

    def on_device(queries, keys, values, lengths, weight):
        tokens = queries.shape[0]
        core = lax.axis_index("grp")
        shard = lax.axis_index("sx") * sy + lax.axis_index("sy")
        stacked = jnp.stack([keys[:, 0], values[:, 0]])
        mine = jnp.concatenate([fetch_behind(stacked, 1, n_srv), fetch_behind(stacked, 2, n_srv)], axis=1)
        weight = lax.ppermute(weight[0], ALL, to_ring)
        mine, weight = lax.optimization_barrier((mine, weight))
        columns = lax.all_gather(weight, "sy", axis=0, tiled=True)
        columns = columns.reshape(2, ZL * n_grp, weight.shape[0], weight.shape[1])

        def gather_heads(queries, stacked, mine, lengths):
            window = jnp.concatenate([mine, lax.ppermute(mine, "grp", [(0, 1), (1, 0)]), stacked], axis=1)
            behind = jnp.stack([1 + 2 * core, 2 + 2 * core, 3 - 2 * core, 4 - 2 * core, 0 * core])
            query_pos = shard * tokens + jnp.arange(tokens, dtype=jnp.int32)
            key_pos = ((shard - behind) * tokens)[:, None] + jnp.arange(tokens, dtype=jnp.int32)[None, :]
            heads = attend(queries, window[0], window[1], query_pos, key_pos.reshape(-1), lengths)
            pair = lax.ppermute(heads, "zl", [(0, 1), (1, 0)])
            parts = []
            for part in (heads, pair):
                own = lax.all_to_all(jnp.broadcast_to(part, (SX,) + part.shape), "sx", 0, 0)
                parts += [own, lax.ppermute(own, "grp", [(0, 1), (1, 0)])]
            return tuple(parts)

        def nothing(queries, stacked, mine, lengths):
            return (jnp.zeros((SX,) + queries.shape, queries.dtype),) * (ZL * n_grp)

        parts = lax.cond(lengths[0] > 0, gather_heads, nothing, queries[:, 0], stacked, mine, lengths)
        turn = lax.axis_index("zh")
        tiles = []
        for t in range(SX):
            tiles.append(lax.ppermute(product((turn + t) % SX, parts, columns), ALL, to_owner[t]))
        return sum(tile.astype(jnp.float32) for tile in tiles).astype(jnp.bfloat16)

    q = P(("sx", "sy"), ("zh", "zl"), "grp")
    k = P(("sx", "sy"), ("zh", "zl"), None)
    placed = (q, k, k, P(), P(("zh", "zl"), "grp", ("sx", "sy")))
    return jax.shard_map(
        on_device, mesh=fine, in_specs=placed, out_specs=P(("sx", "sy"), ("grp", "zh", "zl")), check_vma=False
    )
```

```python
import math

import jax
import jax.numpy as jnp
from jax import lax
from jax.experimental import pallas as pl
from jax.experimental.pallas import tpu as pltpu
from jax.sharding import PartitionSpec as P

REACH = 4
ALL = ("grp", "kv", "sx", "sy")
SX = 4


def doc_starts(lengths, position):
    count = lengths.shape[0]
    before = jnp.arange(count)[None, :] < jnp.arange(count)[:, None]
    starts = jnp.sum(jnp.where(before, lengths[None, :], 0), axis=1)
    chosen = jnp.where(starts[None, :] <= position[:, None], starts[None, :], 0)
    return jnp.max(chosen, axis=1)


def attend(queries, window_keys, window_values, query_pos, key_pos, lengths):
    token_count = queries.shape[0]
    head_size = window_keys.shape[1]
    heads = queries.shape[1] // head_size
    split = queries.reshape(token_count, heads, head_size)
    scores = jnp.einsum("thd,wd->htw", split, window_keys, preferred_element_type=jnp.float32)
    scores = scores * (1.0 / math.sqrt(head_size))
    first_key = doc_starts(lengths, query_pos)
    allowed = (key_pos[None, :] >= first_key[:, None]) & (key_pos[None, :] <= query_pos[:, None])
    scores = jnp.where(allowed[None], scores, -jnp.inf)
    peak = jnp.max(scores, axis=2, keepdims=True)
    weights = jnp.exp(scores - peak)
    total = jnp.sum(weights, axis=2)
    numer = jnp.einsum(
        "htw,wd->thd", weights.astype(jnp.bfloat16), window_values, preferred_element_type=jnp.float32
    )
    result = numer / jnp.transpose(total, (1, 0))[..., None]
    return result.astype(jnp.bfloat16).reshape(token_count, heads * head_size)


def fetch_behind(stacked, near, n_srv):
    route = []
    for c in range(2):
        distance = near + 2 * c
        route += [(c * n_srv + i - distance, c * n_srv + i) for i in range(distance, n_srv)]
    return lax.ppermute(stacked, ("grp", "sx", "sy"), route)


def product_kernel(place_ref, left_ref, right_ref, out_ref):
    rows, _, cores, tokens, depth = left_ref.shape
    left = jnp.concatenate(
        [jnp.concatenate([left_ref[h, 0, c] for c in range(cores)], axis=1) for h in range(rows)], axis=0
    )
    pieces, _, _, width = right_ref.shape
    for piece in range(pieces):
        total = jnp.dot(
            left, right_ref[piece].reshape(cores * depth, width), preferred_element_type=jnp.float32
        ).astype(out_ref.dtype)
        for h in range(rows):
            out_ref[h, :, piece * width : (piece + 1) * width] = total[h * tokens : (h + 1) * tokens]


def product(place, left, right):
    rows, _, cores, tokens, depth = left.shape
    pieces, _, _, width = right.shape
    tiles = pieces // 2
    grid_spec = pltpu.PrefetchScalarGridSpec(
        num_scalar_prefetch=1,
        grid=(tiles,),
        in_specs=[
            pl.BlockSpec((rows, 1, cores, tokens, depth), lambda j, place: (0, place[0], 0, 0, 0)),
            pl.BlockSpec((2, cores, depth, width), lambda j, place: (j, 0, 0, 0)),
        ],
        out_specs=pl.BlockSpec((rows, tokens, 2 * width), lambda j, place: ((j + place[1]) % tiles, 0, 0)),
    )
    return pl.pallas_call(
        product_kernel,
        grid_spec=grid_spec,
        out_shape=jax.ShapeDtypeStruct((tiles * rows, tokens, 2 * width), jnp.bfloat16),
        compiler_params=pltpu.CompilerParams(vmem_limit_bytes=58 * 2**20),
        cost_estimate=pl.CostEstimate(
            flops=2 * rows * tokens * right.size,
            bytes_accessed=2 * (left.size // 2 + right.size + tiles * rows * tokens * 2 * width),
            transcendentals=0,
        ),
    )(place, left, right)


def solution(mesh):
    n_grp, n_kv, n_srv = mesh.shape["grp"], mesh.shape["kv"], mesh.shape["srv"]
    sy = n_srv // SX
    sizes = (n_grp, n_kv, SX, sy)
    fine = jax.sharding.Mesh(mesh.devices.reshape(sizes), ALL)
    tiles = n_grp * n_kv // SX

    def index(*place):
        total = 0
        for at, size in zip(place, sizes):
            total = total * size + at
        return total

    def shift_of(x):
        return tiles - 1 + (x % 2) * (tiles // 2)

    to_owner = [[], []]
    for t in range(2):
        for c in range(n_grp):
            for z in range(n_kv):
                for x in range(SX):
                    j = (z // 2 - shift_of(x)) % tiles
                    to_x = 2 * (z % 2) + (c ^ t)
                    owner = x * tiles + j
                    for y in range(sy):
                        to_owner[t].append(
                            (index(c, z, x, y), index(owner // n_kv, owner % n_kv, to_x, y))
                        )

    def on_device(queries, keys, values, lengths, weight):
        tokens = queries.shape[0]
        core = lax.axis_index("grp")
        across = lax.axis_index("sx")
        shard = across * sy + lax.axis_index("sy")
        columns = lax.all_gather(weight[0], ("sy", "grp"), axis=0, tiled=True)
        columns = columns.reshape(sy, n_grp, weight.shape[1], weight.shape[2])

        stacked = jnp.stack([keys[:, 0], values[:, 0]])
        mine = jnp.concatenate([fetch_behind(stacked, 1, n_srv), fetch_behind(stacked, 2, n_srv)], axis=1)
        window = jnp.concatenate([mine, lax.ppermute(mine, "grp", [(0, 1), (1, 0)]), stacked], axis=1)
        behind = jnp.stack([1 + 2 * core, 2 + 2 * core, 3 - 2 * core, 4 - 2 * core, 0 * core])
        query_pos = shard * tokens + jnp.arange(tokens, dtype=jnp.int32)
        key_pos = ((shard - behind) * tokens)[:, None] + jnp.arange(tokens, dtype=jnp.int32)[None, :]
        heads = attend(queries[:, 0], window[0], window[1], query_pos, key_pos.reshape(-1), lengths)
        heads = lax.all_to_all(heads.reshape(n_grp, tokens // n_grp, heads.shape[1]), "grp", 0, 0)
        along = lax.all_to_all(jnp.broadcast_to(heads, (SX,) + heads.shape), "sx", 0, 0)
        along = along.reshape((SX // 2, 2) + heads.shape)

        partial = [product(jnp.stack([core ^ t, shift_of(across)]), along, columns) for t in range(2)]
        late = lax.psum_scatter(partial[1], "kv", scatter_dimension=0, tiled=True)[0]
        early = lax.all_to_all(partial[0], "kv", 0, 0, tiled=True)
        early = jnp.sum(early.astype(jnp.float32), axis=0).astype(jnp.bfloat16)
        early = lax.ppermute(early, ALL, to_owner[0])
        late = lax.ppermute(late, ALL, to_owner[1])
        even = across % 2 == 0
        return jnp.concatenate([jnp.where(even, early, late), jnp.where(even, late, early)], axis=0)

    q = P(("sx", "sy"), "kv", "grp")
    k = P(("sx", "sy"), "kv", None)
    placed = (q, k, k, P(), P("kv", "grp", ("sx", "sy")))
    return jax.shard_map(
        on_device, mesh=fine, in_specs=placed, out_specs=P(("sx", "sy"), ("grp", "kv")), check_vma=False
    )
```

```python
import functools
import math

import jax
import jax.numpy as jnp
from jax import lax
from jax.experimental import pallas as pl
from jax.experimental.pallas import tpu as pltpu
from jax.sharding import PartitionSpec as P

REACH = 4
ALL = ("grp", "kv", "sx", "sy")
SX = 4


def doc_starts(lengths, position):
    count = lengths.shape[0]
    before = jnp.arange(count)[None, :] < jnp.arange(count)[:, None]
    starts = jnp.sum(jnp.where(before, lengths[None, :], 0), axis=1)
    chosen = jnp.where(starts[None, :] <= position[:, None], starts[None, :], 0)
    return jnp.max(chosen, axis=1)


def attend(queries, window_keys, window_values, query_pos, key_pos, lengths):
    token_count = queries.shape[0]
    head_size = window_keys.shape[1]
    heads = queries.shape[1] // head_size
    split = queries.reshape(token_count, heads, head_size)
    scores = jnp.einsum("thd,wd->htw", split, window_keys, preferred_element_type=jnp.float32)
    scores = scores * (1.0 / math.sqrt(head_size))
    first_key = doc_starts(lengths, query_pos)
    allowed = (key_pos[None, :] >= first_key[:, None]) & (key_pos[None, :] <= query_pos[:, None])
    scores = jnp.where(allowed[None], scores, -jnp.inf)
    peak = jnp.max(scores, axis=2, keepdims=True)
    weights = jnp.exp(scores - peak)
    total = jnp.sum(weights, axis=2)
    numer = jnp.einsum(
        "htw,wd->thd", weights.astype(jnp.bfloat16), window_values, preferred_element_type=jnp.float32
    )
    result = numer / jnp.transpose(total, (1, 0))[..., None]
    return result.astype(jnp.bfloat16).reshape(token_count, heads * head_size)


def fetch_behind(stacked, near, n_srv):
    route = []
    for c in range(2):
        distance = near + 2 * c
        route += [(c * n_srv + i - distance, c * n_srv + i) for i in range(distance, n_srv)]
    return lax.ppermute(stacked, ("grp", "sx", "sy"), route)


def product_kernel(place_ref, left_ref, *refs):
    *right_refs, out_ref = refs
    rows, _, cores, tokens, depth = left_ref.shape
    left = jnp.concatenate(
        [jnp.concatenate([left_ref[h, 0, c] for c in range(cores)], axis=1) for h in range(rows)], axis=0
    )
    for piece in range(2):
        right = jnp.concatenate([right_refs[piece * cores + c][0, 0] for c in range(cores)], axis=0)
        width = right.shape[1]
        total = jnp.dot(left, right, preferred_element_type=jnp.float32).astype(out_ref.dtype)
        for h in range(rows):
            out_ref[h, :, piece * width : (piece + 1) * width] = total[h * tokens : (h + 1) * tokens]


def product(place, left, right):
    rows, _, cores, tokens, depth = left.shape
    pieces, _, _, width = right.shape
    tiles = pieces // 2
    grid_spec = pltpu.PrefetchScalarGridSpec(
        num_scalar_prefetch=1,
        grid=(tiles,),
        in_specs=[
            pl.BlockSpec((rows, 1, cores, tokens, depth), lambda j, place: (0, place[0], 0, 0, 0)),
        ]
        + [
            pl.BlockSpec((1, 1, depth, width), functools.partial(lambda p, c, j, place: (2 * j + p, c, 0, 0), p, c))
            for p in range(2)
            for c in range(cores)
        ],
        out_specs=pl.BlockSpec((rows, tokens, 2 * width), lambda j, place: ((j + place[1]) % tiles, 0, 0)),
    )
    return pl.pallas_call(
        product_kernel,
        grid_spec=grid_spec,
        out_shape=jax.ShapeDtypeStruct((tiles * rows, tokens, 2 * width), jnp.bfloat16),
        compiler_params=pltpu.CompilerParams(vmem_limit_bytes=58 * 2**20),
        cost_estimate=pl.CostEstimate(
            flops=2 * rows * tokens * right.size,
            bytes_accessed=2 * (left.size // 2 + right.size + tiles * rows * tokens * 2 * width),
            transcendentals=0,
        ),
    )(place, left, *[right] * (2 * cores))


def solution(mesh):
    n_grp, n_kv, n_srv = mesh.shape["grp"], mesh.shape["kv"], mesh.shape["srv"]
    sy = n_srv // SX
    sizes = (n_grp, n_kv, SX, sy)
    fine = jax.sharding.Mesh(mesh.devices.reshape(sizes), ALL)
    tiles = n_grp * n_kv // SX

    def index(*place):
        total = 0
        for at, size in zip(place, sizes):
            total = total * size + at
        return total

    def shift_of(x):
        return tiles - 1 + (x % 2) * (tiles // 2)

    to_owner = [[], []]
    for t in range(2):
        for c in range(n_grp):
            for z in range(n_kv):
                for x in range(SX):
                    j = (z // 2 - shift_of(x)) % tiles
                    to_x = 2 * (z % 2) + (c ^ t)
                    owner = x * tiles + j
                    for y in range(sy):
                        to_owner[t].append(
                            (index(c, z, x, y), index(owner // n_kv, owner % n_kv, to_x, y))
                        )

    def on_device(queries, keys, values, lengths, weight):
        tokens = queries.shape[0]
        core = lax.axis_index("grp")
        across = lax.axis_index("sx")
        shard = across * sy + lax.axis_index("sy")
        columns = lax.all_gather(weight[0], ("sy", "grp"), axis=0, tiled=True)
        columns = columns.reshape(sy, n_grp, weight.shape[1], weight.shape[2])

        stacked = jnp.stack([keys[:, 0], values[:, 0]])
        mine = jnp.concatenate([fetch_behind(stacked, 1, n_srv), fetch_behind(stacked, 2, n_srv)], axis=1)
        window = jnp.concatenate([mine, lax.ppermute(mine, "grp", [(0, 1), (1, 0)]), stacked], axis=1)
        behind = jnp.stack([1 + 2 * core, 2 + 2 * core, 3 - 2 * core, 4 - 2 * core, 0 * core])
        query_pos = shard * tokens + jnp.arange(tokens, dtype=jnp.int32)
        key_pos = ((shard - behind) * tokens)[:, None] + jnp.arange(tokens, dtype=jnp.int32)[None, :]
        heads = attend(queries[:, 0], window[0], window[1], query_pos, key_pos.reshape(-1), lengths)
        heads = lax.all_to_all(heads.reshape(n_grp, tokens // n_grp, heads.shape[1]), "grp", 0, 0)
        along = lax.all_to_all(jnp.broadcast_to(heads, (SX,) + heads.shape), "sx", 0, 0)
        along = along.reshape((SX // 2, 2) + heads.shape)

        partial = [product(jnp.stack([core ^ t, shift_of(across)]), along, columns) for t in range(2)]
        tiles_in = []
        for t in range(2):
            terms = lax.all_to_all(partial[t], "kv", 0, 0, tiled=True)
            tile = jnp.sum(terms.astype(jnp.float32), axis=0).astype(jnp.bfloat16)
            tiles_in.append(lax.ppermute(tile, ALL, to_owner[t]))
        early, late = tiles_in
        even = across % 2 == 0
        return jnp.concatenate([jnp.where(even, early, late), jnp.where(even, late, early)], axis=0)

    q = P(("sx", "sy"), "kv", "grp")
    k = P(("sx", "sy"), "kv", None)
    placed = (q, k, k, P(), P("kv", "grp", ("sx", "sy")))
    return jax.shard_map(
        on_device, mesh=fine, in_specs=placed, out_specs=P(("sx", "sy"), ("grp", "kv")), check_vma=False
    )
```

```python
import math

import jax
import jax.numpy as jnp
from jax import lax
from jax.experimental import pallas as pl
from jax.experimental.pallas import tpu as pltpu
from jax.sharding import PartitionSpec as P

REACH = 4
ALL = ("grp", "kv", "sx", "sy")
SX = 4


def doc_starts(lengths, position):
    count = lengths.shape[0]
    before = jnp.arange(count)[None, :] < jnp.arange(count)[:, None]
    starts = jnp.sum(jnp.where(before, lengths[None, :], 0), axis=1)
    chosen = jnp.where(starts[None, :] <= position[:, None], starts[None, :], 0)
    return jnp.max(chosen, axis=1)


def attend(queries, window_keys, window_values, query_pos, key_pos, lengths):
    token_count = queries.shape[0]
    head_size = window_keys.shape[1]
    heads = queries.shape[1] // head_size
    split = queries.reshape(token_count, heads, head_size)
    scores = jnp.einsum("thd,wd->htw", split, window_keys, preferred_element_type=jnp.float32)
    scores = scores * (1.0 / math.sqrt(head_size))
    first_key = doc_starts(lengths, query_pos)
    allowed = (key_pos[None, :] >= first_key[:, None]) & (key_pos[None, :] <= query_pos[:, None])
    scores = jnp.where(allowed[None], scores, -jnp.inf)
    peak = jnp.max(scores, axis=2, keepdims=True)
    weights = jnp.exp(scores - peak)
    total = jnp.sum(weights, axis=2)
    numer = jnp.einsum(
        "htw,wd->thd", weights.astype(jnp.bfloat16), window_values, preferred_element_type=jnp.float32
    )
    result = numer / jnp.transpose(total, (1, 0))[..., None]
    return result.astype(jnp.bfloat16).reshape(token_count, heads * head_size)


def fetch_behind(stacked, near, n_srv):
    route = []
    for c in range(2):
        distance = near + 2 * c
        route += [(c * n_srv + i - distance, c * n_srv + i) for i in range(distance, n_srv)]
    return lax.ppermute(stacked, ("grp", "sx", "sy"), route)


def product_kernel(place_ref, left_ref, own_ref, other_ref, out_ref):
    blocks, tokens, depth = left_ref.shape
    left = left_ref[...].reshape(blocks * tokens, depth)
    half = depth // 2
    core = place_ref[0]
    for piece in range(own_ref.shape[0]):
        total = jnp.dot(left[:, :half], own_ref[piece, 0], preferred_element_type=jnp.float32)
        total += jnp.dot(left[:, half:], other_ref[piece, 0], preferred_element_type=jnp.float32)
        total = total.astype(out_ref.dtype)
        width = total.shape[1]
        for x in range(blocks):
            out_ref[x // 2, (x % 2) ^ core, :, piece * width : (piece + 1) * width] = total[
                x * tokens : (x + 1) * tokens
            ]


def product(place, left, right):
    blocks, tokens, depth = left.shape
    pieces, _, half, width = right.shape
    tiles = pieces // 2
    grid_spec = pltpu.PrefetchScalarGridSpec(
        num_scalar_prefetch=1,
        grid=(tiles,),
        in_specs=[
            pl.BlockSpec((blocks, tokens, depth), lambda j, place: (0, 0, 0)),
            pl.BlockSpec((2, 1, half, width), lambda j, place: (j, place[0], 0, 0)),
            pl.BlockSpec((2, 1, half, width), lambda j, place: (j, 1 - place[0], 0, 0)),
        ],
        out_specs=pl.BlockSpec(
            (blocks // 2, 2, tokens, 2 * width), lambda j, place: ((j + place[1]) % tiles, 0, 0, 0)
        ),
    )
    return pl.pallas_call(
        product_kernel,
        grid_spec=grid_spec,
        out_shape=jax.ShapeDtypeStruct((tiles * blocks // 2, 2, tokens, 2 * width), jnp.bfloat16),
        compiler_params=pltpu.CompilerParams(vmem_limit_bytes=58 * 2**20),
        cost_estimate=pl.CostEstimate(
            flops=2 * blocks * tokens * right.size,
            bytes_accessed=2 * (left.size + right.size + tiles * blocks * tokens * 2 * width),
            transcendentals=0,
        ),
    )(place, left, right, right)


def solution(mesh):
    n_grp, n_kv, n_srv = mesh.shape["grp"], mesh.shape["kv"], mesh.shape["srv"]
    sy = n_srv // SX
    sizes = (n_grp, n_kv, SX, sy)
    fine = jax.sharding.Mesh(mesh.devices.reshape(sizes), ALL)
    tiles = n_grp * n_kv // SX

    def index(*place):
        total = 0
        for at, size in zip(place, sizes):
            total = total * size + at
        return total

    def shift_of(x):
        return tiles - 1 + (x % 2) * (tiles // 2)

    to_owner = [[], []]
    for t in range(2):
        for c in range(n_grp):
            for z in range(n_kv):
                for x in range(SX):
                    j = (z // 2 - shift_of(x)) % tiles
                    to_x = 2 * (z % 2) + (c ^ t)
                    owner = x * tiles + j
                    for y in range(sy):
                        to_owner[t].append(
                            (index(c, z, x, y), index(owner // n_kv, owner % n_kv, to_x, y))
                        )

    def on_device(queries, keys, values, lengths, weight):
        tokens = queries.shape[0]
        core = lax.axis_index("grp")
        across = lax.axis_index("sx")
        shard = across * sy + lax.axis_index("sy")
        columns = lax.all_gather(weight[0], ("sy", "grp"), axis=0, tiled=True)
        columns = columns.reshape(sy, n_grp, weight.shape[1], weight.shape[2])

        half = tokens // n_grp
        stacked = jnp.stack([keys[:, 0], values[:, 0]])
        mine = jnp.concatenate([fetch_behind(stacked, 1, n_srv), fetch_behind(stacked, 2, n_srv)], axis=1)
        own = lax.dynamic_slice_in_dim(queries[:, 0], core * half, half, 0)
        other = lax.dynamic_slice_in_dim(queries[:, 0], (1 - core) * half, half, 0)
        other = lax.ppermute(other, "grp", [(0, 1), (1, 0)])
        window = jnp.concatenate([mine, lax.ppermute(mine, "grp", [(0, 1), (1, 0)]), stacked], axis=1)
        behind = jnp.stack([1 + 2 * core, 2 + 2 * core, 3 - 2 * core, 4 - 2 * core, 0 * core])
        query_pos = shard * tokens + core * half + jnp.arange(half, dtype=jnp.int32)
        key_pos = ((shard - behind) * tokens)[:, None] + jnp.arange(tokens, dtype=jnp.int32)[None, :]
        both = jnp.concatenate([own, other], axis=1)
        heads = attend(both, window[0], window[1], query_pos, key_pos.reshape(-1), lengths)
        along = lax.all_to_all(jnp.broadcast_to(heads, (SX,) + heads.shape), "sx", 0, 0)

        partial = product(jnp.stack([core, shift_of(across)]), along, columns)
        partial = partial.reshape(n_kv * 2 * half, partial.shape[3])
        summed = lax.psum_scatter(partial, "kv", scatter_dimension=0, tiled=True).reshape(2, half, -1)
        early, late = [lax.ppermute(summed[t], ALL, to_owner[t]) for t in range(2)]
        even = across % 2 == 0
        return jnp.concatenate([jnp.where(even, early, late), jnp.where(even, late, early)], axis=0)

    q = P(("sx", "sy"), "kv", "grp")
    k = P(("sx", "sy"), "kv", None)
    placed = (q, k, k, P(), P("kv", "grp", ("sx", "sy")))
    return jax.shard_map(
        on_device, mesh=fine, in_specs=placed, out_specs=P(("sx", "sy"), ("grp", "kv")), check_vma=False
    )
```

```python
import math

import jax
import jax.numpy as jnp
from jax import lax
from jax.experimental import pallas as pl
from jax.experimental.pallas import tpu as pltpu
from jax.sharding import PartitionSpec as P

REACH = 4
ALL = ("grp", "kv", "sx", "sy")
SX = 4


def doc_starts(lengths, position):
    count = lengths.shape[0]
    before = jnp.arange(count)[None, :] < jnp.arange(count)[:, None]
    starts = jnp.sum(jnp.where(before, lengths[None, :], 0), axis=1)
    chosen = jnp.where(starts[None, :] <= position[:, None], starts[None, :], 0)
    return jnp.max(chosen, axis=1)


def attend(queries, window_keys, window_values, query_pos, key_pos, lengths):
    token_count = queries.shape[0]
    head_size = window_keys.shape[1]
    heads = queries.shape[1] // head_size
    split = queries.reshape(token_count, heads, head_size)
    scores = jnp.einsum("thd,wd->htw", split, window_keys, preferred_element_type=jnp.float32)
    scores = scores * (1.0 / math.sqrt(head_size))
    first_key = doc_starts(lengths, query_pos)
    allowed = (key_pos[None, :] >= first_key[:, None]) & (key_pos[None, :] <= query_pos[:, None])
    scores = jnp.where(allowed[None], scores, -jnp.inf)
    peak = jnp.max(scores, axis=2, keepdims=True)
    weights = jnp.exp(scores - peak)
    total = jnp.sum(weights, axis=2)
    numer = jnp.einsum(
        "htw,wd->thd", weights.astype(jnp.bfloat16), window_values, preferred_element_type=jnp.float32
    )
    result = numer / jnp.transpose(total, (1, 0))[..., None]
    return result.astype(jnp.bfloat16).reshape(token_count, heads * head_size)


def fetch_behind(stacked, near, n_srv):
    route = []
    for c in range(2):
        distance = near + 2 * c
        route += [(c * n_srv + i - distance, c * n_srv + i) for i in range(distance, n_srv)]
    return lax.ppermute(stacked, ("grp", "sx", "sy"), route)


def product_kernel(place_ref, left_ref, right_ref, out_ref):
    blocks, tokens, depth = left_ref.shape
    left = left_ref[...].reshape(blocks * tokens, depth)
    core = place_ref[0]
    pieces, _, _, width = right_ref.shape
    for piece in range(pieces):
        total = jnp.dot(
            left, right_ref[piece].reshape(depth, width), preferred_element_type=jnp.float32
        ).astype(out_ref.dtype)
        for x in range(blocks):
            out_ref[x // 2, (x % 2) ^ core, :, piece * width : (piece + 1) * width] = total[
                x * tokens : (x + 1) * tokens
            ]


def product(place, left, right):
    blocks, tokens, depth = left.shape
    pieces, cores, half, width = right.shape
    tiles = pieces // 2
    grid_spec = pltpu.PrefetchScalarGridSpec(
        num_scalar_prefetch=1,
        grid=(tiles,),
        in_specs=[
            pl.BlockSpec(memory_space=pltpu.VMEM),
            pl.BlockSpec((2, cores, half, width), lambda j, place: (j, 0, 0, 0)),
        ],
        out_specs=pl.BlockSpec(
            (blocks // 2, 2, tokens, 2 * width), lambda j, place: ((j + place[1]) % tiles, 0, 0, 0)
        ),
    )
    return pl.pallas_call(
        product_kernel,
        grid_spec=grid_spec,
        out_shape=jax.ShapeDtypeStruct((tiles * blocks // 2, 2, tokens, 2 * width), jnp.bfloat16),
        compiler_params=pltpu.CompilerParams(vmem_limit_bytes=40 * 2**20),
        cost_estimate=pl.CostEstimate(
            flops=2 * blocks * tokens * right.size,
            bytes_accessed=2 * (left.size + right.size + tiles * blocks * tokens * 2 * width),
            transcendentals=0,
        ),
    )(place, left, right)


def solution(mesh):
    n_grp, n_kv, n_srv = mesh.shape["grp"], mesh.shape["kv"], mesh.shape["srv"]
    sy = n_srv // SX
    sizes = (n_grp, n_kv, SX, sy)
    fine = jax.sharding.Mesh(mesh.devices.reshape(sizes), ALL)
    tiles = n_grp * n_kv // SX

    def index(*place):
        total = 0
        for at, size in zip(place, sizes):
            total = total * size + at
        return total

    def shift_of(x):
        return tiles - 1 + (x % 2) * (tiles // 2)

    to_owner = [[], []]
    for t in range(2):
        for c in range(n_grp):
            for z in range(n_kv):
                for x in range(SX):
                    j = (z // 2 - shift_of(x)) % tiles
                    to_x = 2 * (z % 2) + (c ^ t)
                    owner = x * tiles + j
                    for y in range(sy):
                        to_owner[t].append(
                            (index(c, z, x, y), index(owner // n_kv, owner % n_kv, to_x, y))
                        )

    def on_device(queries, keys, values, lengths, weight):
        tokens = queries.shape[0]
        core = lax.axis_index("grp")
        across = lax.axis_index("sx")
        shard = across * sy + lax.axis_index("sy")
        columns = lax.all_gather(weight[0], ("sy", "grp"), axis=0, tiled=True)
        columns = columns.reshape(sy, n_grp, weight.shape[1], weight.shape[2])

        half = tokens // n_grp
        stacked = jnp.stack([keys[:, 0], values[:, 0]])
        mine = jnp.concatenate([fetch_behind(stacked, 1, n_srv), fetch_behind(stacked, 2, n_srv)], axis=1)
        own = lax.dynamic_slice_in_dim(queries[:, 0], core * half, half, 0)
        other = lax.dynamic_slice_in_dim(queries[:, 0], (1 - core) * half, half, 0)
        other = lax.ppermute(other, "grp", [(0, 1), (1, 0)])
        window = jnp.concatenate([mine, lax.ppermute(mine, "grp", [(0, 1), (1, 0)]), stacked], axis=1)
        behind = jnp.stack([1 + 2 * core, 2 + 2 * core, 3 - 2 * core, 4 - 2 * core, 0 * core])
        query_pos = shard * tokens + core * half + jnp.arange(half, dtype=jnp.int32)
        key_pos = ((shard - behind) * tokens)[:, None] + jnp.arange(tokens, dtype=jnp.int32)[None, :]
        first = core == 0
        both = jnp.concatenate([jnp.where(first, own, other), jnp.where(first, other, own)], axis=1)
        heads = attend(both, window[0], window[1], query_pos, key_pos.reshape(-1), lengths)
        along = lax.all_to_all(jnp.broadcast_to(heads, (SX,) + heads.shape), "sx", 0, 0)

        partial = product(jnp.stack([core, shift_of(across)]), along, columns)
        partial = partial.reshape(n_kv, 2 * half, partial.shape[3])
        summed = lax.psum_scatter(partial, "kv", scatter_dimension=0).reshape(2, half, -1)
        early, late = [lax.ppermute(summed[t], ALL, to_owner[t]) for t in range(2)]
        even = across % 2 == 0
        return jnp.concatenate([jnp.where(even, early, late), jnp.where(even, late, early)], axis=0)

    q = P(("sx", "sy"), "kv", "grp")
    k = P(("sx", "sy"), "kv", None)
    placed = (q, k, k, P(), P("kv", "grp", ("sx", "sy")))
    return jax.shard_map(
        on_device, mesh=fine, in_specs=placed, out_specs=P(("sx", "sy"), ("grp", "kv")), check_vma=False
    )
```

```python
import math

import jax
import jax.numpy as jnp
from jax import lax
from jax.experimental import pallas as pl
from jax.experimental.pallas import tpu as pltpu
from jax.sharding import PartitionSpec as P

REACH = 4
ALL = ("grp", "kv", "sx", "sy")
SX = 4


def doc_starts(lengths, position):
    count = lengths.shape[0]
    before = jnp.arange(count)[None, :] < jnp.arange(count)[:, None]
    starts = jnp.sum(jnp.where(before, lengths[None, :], 0), axis=1)
    chosen = jnp.where(starts[None, :] <= position[:, None], starts[None, :], 0)
    return jnp.max(chosen, axis=1)


def attend(queries, window_keys, window_values, query_pos, key_pos, lengths):
    token_count = queries.shape[0]
    head_size = window_keys.shape[1]
    heads = queries.shape[1] // head_size
    split = queries.reshape(token_count, heads, head_size)
    scores = jnp.einsum("thd,wd->htw", split, window_keys, preferred_element_type=jnp.float32)
    scores = scores * (1.0 / math.sqrt(head_size))
    first_key = doc_starts(lengths, query_pos)
    allowed = (key_pos[None, :] >= first_key[:, None]) & (key_pos[None, :] <= query_pos[:, None])
    scores = jnp.where(allowed[None], scores, -jnp.inf)
    peak = jnp.max(scores, axis=2, keepdims=True)
    weights = jnp.exp(scores - peak)
    total = jnp.sum(weights, axis=2)
    numer = jnp.einsum(
        "htw,wd->thd", weights.astype(jnp.bfloat16), window_values, preferred_element_type=jnp.float32
    )
    result = numer / jnp.transpose(total, (1, 0))[..., None]
    return result.astype(jnp.bfloat16).reshape(token_count, heads * head_size)


def fetch_behind(stacked, near, n_srv):
    route = []
    for c in range(2):
        distance = near + 2 * c
        route += [(c * n_srv + i - distance, c * n_srv + i) for i in range(distance, n_srv)]
    return lax.ppermute(stacked, ("grp", "sx", "sy"), route)


def product_kernel(place_ref, left_ref, right_ref, out_ref):
    blocks, tokens, depth = left_ref.shape
    left = left_ref[...].reshape(blocks * tokens, depth)
    core, across = place_ref[0], place_ref[2]
    pieces, _, _, width = right_ref.shape
    for piece in range(pieces):
        total = jnp.dot(
            left, right_ref[piece].reshape(depth, width), preferred_element_type=jnp.float32
        ).astype(out_ref.dtype)
        for x in range(blocks):
            ahead = (x + blocks - across) % blocks
            out_ref[ahead // 2, (ahead % 2) ^ core, :, piece * width : (piece + 1) * width] = total[
                x * tokens : (x + 1) * tokens
            ]


def product(place, left, right):
    blocks, tokens, depth = left.shape
    pieces, cores, half, width = right.shape
    tiles = pieces // 2
    grid_spec = pltpu.PrefetchScalarGridSpec(
        num_scalar_prefetch=1,
        grid=(tiles,),
        in_specs=[
            pl.BlockSpec(memory_space=pltpu.VMEM),
            pl.BlockSpec((2, cores, half, width), lambda j, place: (j, 0, 0, 0)),
        ],
        out_specs=pl.BlockSpec(
            (blocks // 2, 2, tokens, 2 * width), lambda j, place: ((j + place[1]) % tiles, 0, 0, 0)
        ),
    )
    return pl.pallas_call(
        product_kernel,
        grid_spec=grid_spec,
        out_shape=jax.ShapeDtypeStruct((tiles * blocks // 2, 2, tokens, 2 * width), jnp.bfloat16),
        compiler_params=pltpu.CompilerParams(vmem_limit_bytes=40 * 2**20),
        cost_estimate=pl.CostEstimate(
            flops=2 * blocks * tokens * right.size,
            bytes_accessed=2 * (left.size + right.size + tiles * blocks * tokens * 2 * width),
            transcendentals=0,
        ),
    )(place, left, right)


def solution(mesh):
    n_grp, n_kv, n_srv = mesh.shape["grp"], mesh.shape["kv"], mesh.shape["srv"]
    sy = n_srv // SX
    sizes = (n_grp, n_kv, SX, sy)
    fine = jax.sharding.Mesh(mesh.devices.reshape(sizes), ALL)
    tiles = n_grp * n_kv // SX

    def index(*place):
        total = 0
        for at, size in zip(place, sizes):
            total = total * size + at
        return total

    def shift_of(x):
        return tiles - 1 + (x % 2) * (tiles // 2)

    to_owner = [[], []]
    for t in range(2):
        for c in range(n_grp):
            for z in range(n_kv):
                for x in range(SX):
                    j = (z // 2 - shift_of(x)) % tiles
                    to_x = (x + 2 * (z % 2) + (c ^ t)) % SX
                    owner = x * tiles + j
                    for y in range(sy):
                        to_owner[t].append(
                            (index(c, z, x, y), index(owner // n_kv, owner % n_kv, to_x, y))
                        )

    def on_device(queries, keys, values, lengths, weight):
        tokens = queries.shape[0]
        core = lax.axis_index("grp")
        across = lax.axis_index("sx")
        shard = across * sy + lax.axis_index("sy")
        columns = lax.all_gather(weight[0], ("sy", "grp"), axis=0, tiled=True)
        columns = columns.reshape(sy, n_grp, weight.shape[1], weight.shape[2])

        half = tokens // n_grp
        stacked = jnp.stack([keys[:, 0], values[:, 0]])
        mine = jnp.concatenate([fetch_behind(stacked, 1, n_srv), fetch_behind(stacked, 2, n_srv)], axis=1)
        own = lax.dynamic_slice_in_dim(queries[:, 0], core * half, half, 0)
        other = lax.dynamic_slice_in_dim(queries[:, 0], (1 - core) * half, half, 0)
        other = lax.ppermute(other, "grp", [(0, 1), (1, 0)])
        window = jnp.concatenate([mine, lax.ppermute(mine, "grp", [(0, 1), (1, 0)]), stacked], axis=1)
        behind = jnp.stack([1 + 2 * core, 2 + 2 * core, 3 - 2 * core, 4 - 2 * core, 0 * core])
        query_pos = shard * tokens + core * half + jnp.arange(half, dtype=jnp.int32)
        key_pos = ((shard - behind) * tokens)[:, None] + jnp.arange(tokens, dtype=jnp.int32)[None, :]
        first = core == 0
        both = jnp.concatenate([jnp.where(first, own, other), jnp.where(first, other, own)], axis=1)
        heads = attend(both, window[0], window[1], query_pos, key_pos.reshape(-1), lengths)
        along = lax.all_to_all(jnp.broadcast_to(heads, (SX,) + heads.shape), "sx", 0, 0)

        partial = product(jnp.stack([core, shift_of(across), across]), along, columns)
        partial = partial.reshape(n_kv, 2 * half, partial.shape[3])
        summed = lax.psum_scatter(partial, "kv", scatter_dimension=0).reshape(2, half, -1)
        early, late = [lax.ppermute(summed[t], ALL, to_owner[t]) for t in range(2)]
        even = (across + lax.axis_index("kv") // tiles) % 2 == 0
        return jnp.concatenate([jnp.where(even, early, late), jnp.where(even, late, early)], axis=0)

    q = P(("sx", "sy"), "kv", "grp")
    k = P(("sx", "sy"), "kv", None)
    placed = (q, k, k, P(), P("kv", "grp", ("sx", "sy")))
    return jax.shard_map(
        on_device, mesh=fine, in_specs=placed, out_specs=P(("sx", "sy"), ("grp", "kv")), check_vma=False
    )
```

```python
import math

import jax
import jax.numpy as jnp
from jax import lax
from jax.experimental import pallas as pl
from jax.experimental.pallas import tpu as pltpu
from jax.sharding import PartitionSpec as P

REACH = 4
ALL = ("grp", "kv", "sx", "sy")
SX = 4


def doc_starts(lengths, position):
    count = lengths.shape[0]
    before = jnp.arange(count)[None, :] < jnp.arange(count)[:, None]
    starts = jnp.sum(jnp.where(before, lengths[None, :], 0), axis=1)
    chosen = jnp.where(starts[None, :] <= position[:, None], starts[None, :], 0)
    return jnp.max(chosen, axis=1)


def attend(queries, window_keys, window_values, query_pos, key_pos, lengths):
    token_count = queries.shape[0]
    head_size = window_keys.shape[1]
    heads = queries.shape[1] // head_size
    split = queries.reshape(token_count, heads, head_size)
    scores = jnp.einsum("thd,wd->htw", split, window_keys, preferred_element_type=jnp.float32)
    scores = scores * (1.0 / math.sqrt(head_size))
    first_key = doc_starts(lengths, query_pos)
    allowed = (key_pos[None, :] >= first_key[:, None]) & (key_pos[None, :] <= query_pos[:, None])
    scores = jnp.where(allowed[None], scores, -jnp.inf)
    peak = jnp.max(scores, axis=2, keepdims=True)
    weights = jnp.exp(scores - peak)
    total = jnp.sum(weights, axis=2)
    numer = jnp.einsum(
        "htw,wd->thd", weights.astype(jnp.bfloat16), window_values, preferred_element_type=jnp.float32
    )
    result = numer / jnp.transpose(total, (1, 0))[..., None]
    return result.astype(jnp.bfloat16).reshape(token_count, heads * head_size)


def fetch_behind(stacked, near, n_srv):
    route = []
    for c in range(2):
        distance = near + 2 * c
        route += [(c * n_srv + i - distance, c * n_srv + i) for i in range(distance, n_srv)]
    return lax.ppermute(stacked, ("grp", "sx", "sy"), route)


def product_kernel(place_ref, left_ref, right_ref, out_ref):
    blocks, tokens, depth = left_ref.shape
    left = left_ref[...].reshape(blocks * tokens, depth)
    core = place_ref[0]
    pieces, _, _, width = right_ref.shape
    for piece in range(pieces):
        total = jnp.dot(
            left, right_ref[piece].reshape(depth, width), preferred_element_type=jnp.float32
        ).astype(out_ref.dtype)
        for x in range(blocks):
            out_ref[x // 2, (x % 2) ^ core, :, piece * width : (piece + 1) * width] = total[
                x * tokens : (x + 1) * tokens
            ]


def product(place, left, right):
    blocks, tokens, depth = left.shape
    pieces, cores, half, width = right.shape
    tiles = pieces // 2
    grid_spec = pltpu.PrefetchScalarGridSpec(
        num_scalar_prefetch=1,
        grid=(tiles,),
        in_specs=[
            pl.BlockSpec(memory_space=pltpu.VMEM),
            pl.BlockSpec((2, cores, half, width), lambda j, place: (j, 0, 0, 0)),
        ],
        out_specs=pl.BlockSpec(
            (blocks // 2, 2, tokens, 2 * width), lambda j, place: ((j + place[1]) % tiles, 0, 0, 0)
        ),
    )
    return pl.pallas_call(
        product_kernel,
        grid_spec=grid_spec,
        out_shape=jax.ShapeDtypeStruct((tiles * blocks // 2, 2, tokens, 2 * width), jnp.bfloat16),
        compiler_params=pltpu.CompilerParams(vmem_limit_bytes=40 * 2**20),
        cost_estimate=pl.CostEstimate(
            flops=2 * blocks * tokens * right.size,
            bytes_accessed=2 * (left.size + right.size + tiles * blocks * tokens * 2 * width),
            transcendentals=0,
        ),
    )(place, left, right)


def solution(mesh):
    n_grp, n_kv, n_srv = mesh.shape["grp"], mesh.shape["kv"], mesh.shape["srv"]
    sy = n_srv // SX
    sizes = (n_grp, n_kv, SX, sy)
    fine = jax.sharding.Mesh(mesh.devices.reshape(sizes), ALL)
    tiles = n_grp * n_kv // SX

    def index(*place):
        total = 0
        for at, size in zip(place, sizes):
            total = total * size + at
        return total

    def shift_of(x):
        return tiles - 1 + (x % 2) * (tiles // 2)

    to_rows, to_owner = [[] for _ in range(SX)], []
    for c in range(n_grp):
        for x in range(SX):
            for b in range(SX):
                to_rows[b].append(((c ^ (b % 2)) * SX + (x + c + 2 * (b // 2)) % SX, c * SX + x))
            for z in range(n_kv):
                owner = x * tiles + (z // 2 - shift_of(x)) % tiles
                to_x = (x + c + 2 * (z % 2)) % SX
                for y in range(sy):
                    to_owner.append((index(c, z, x, y), index(owner // n_kv, owner % n_kv, to_x, y)))

    def on_device(queries, keys, values, lengths, weight):
        tokens = queries.shape[0]
        core = lax.axis_index("grp")
        across = lax.axis_index("sx")
        shard = across * sy + lax.axis_index("sy")
        columns = lax.all_gather(weight[0], ("sy", "grp"), axis=0, tiled=True)
        columns = columns.reshape(sy, n_grp, weight.shape[1], weight.shape[2])

        half = tokens // n_grp
        stacked = jnp.stack([keys[:, 0], values[:, 0]])
        mine = jnp.concatenate([fetch_behind(stacked, 1, n_srv), fetch_behind(stacked, 2, n_srv)], axis=1)
        own = lax.dynamic_slice_in_dim(queries[:, 0], core * half, half, 0)
        other = lax.dynamic_slice_in_dim(queries[:, 0], (1 - core) * half, half, 0)
        other = lax.ppermute(other, "grp", [(0, 1), (1, 0)])
        window = jnp.concatenate([mine, lax.ppermute(mine, "grp", [(0, 1), (1, 0)]), stacked], axis=1)
        behind = jnp.stack([1 + 2 * core, 2 + 2 * core, 3 - 2 * core, 4 - 2 * core, 0 * core])
        query_pos = shard * tokens + core * half + jnp.arange(half, dtype=jnp.int32)
        key_pos = ((shard - behind) * tokens)[:, None] + jnp.arange(tokens, dtype=jnp.int32)[None, :]
        first = core == 0
        both = jnp.concatenate([jnp.where(first, own, other), jnp.where(first, other, own)], axis=1)
        heads = attend(both, window[0], window[1], query_pos, key_pos.reshape(-1), lengths)
        along = jnp.stack([lax.ppermute(heads, ("grp", "sx"), to_rows[b]) for b in range(SX)])

        partial = product(jnp.stack([core, shift_of(across)]), along, columns)
        partial = partial.reshape(n_kv, 2 * half, partial.shape[3])
        tile = lax.psum_scatter(partial, "kv", scatter_dimension=0)
        return lax.ppermute(tile, ALL, to_owner)

    q = P(("sx", "sy"), "kv", "grp")
    k = P(("sx", "sy"), "kv", None)
    placed = (q, k, k, P(), P("kv", "grp", ("sx", "sy")))
    return jax.shard_map(
        on_device, mesh=fine, in_specs=placed, out_specs=P(("sx", "sy"), ("grp", "kv")), check_vma=False
    )
```

```python
import math

import jax
import jax.numpy as jnp
from jax import lax
from jax.experimental import pallas as pl
from jax.experimental.pallas import tpu as pltpu
from jax.sharding import PartitionSpec as P

REACH = 4
ALL = ("grp", "kv", "sx", "sy")
SX = 4


def doc_starts(lengths, position):
    count = lengths.shape[0]
    before = jnp.arange(count)[None, :] < jnp.arange(count)[:, None]
    starts = jnp.sum(jnp.where(before, lengths[None, :], 0), axis=1)
    chosen = jnp.where(starts[None, :] <= position[:, None], starts[None, :], 0)
    return jnp.max(chosen, axis=1)


def attend(queries, window_keys, window_values, query_pos, key_pos, lengths):
    token_count = queries.shape[0]
    head_size = window_keys.shape[1]
    heads = queries.shape[1] // head_size
    split = queries.reshape(token_count, heads, head_size)
    scores = jnp.einsum("thd,wd->htw", split, window_keys, preferred_element_type=jnp.float32)
    scores = scores * (1.0 / math.sqrt(head_size))
    first_key = doc_starts(lengths, query_pos)
    allowed = (key_pos[None, :] >= first_key[:, None]) & (key_pos[None, :] <= query_pos[:, None])
    scores = jnp.where(allowed[None], scores, -jnp.inf)
    peak = jnp.max(scores, axis=2, keepdims=True)
    weights = jnp.exp(scores - peak)
    total = jnp.sum(weights, axis=2)
    numer = jnp.einsum(
        "htw,wd->thd", weights.astype(jnp.bfloat16), window_values, preferred_element_type=jnp.float32
    )
    result = numer / jnp.transpose(total, (1, 0))[..., None]
    return result.astype(jnp.bfloat16).reshape(token_count, heads * head_size)


def fetch_behind(stacked, near, n_srv):
    route = []
    for c in range(2):
        distance = near + 2 * c
        route += [(c * n_srv + i - distance, c * n_srv + i) for i in range(distance, n_srv)]
    return lax.ppermute(stacked, ("grp", "sx", "sy"), route)


def product_kernel(place_ref, left_ref, right_ref, out_ref):
    blocks, tokens, depth = left_ref.shape
    left = left_ref[...].reshape(blocks * tokens, depth)
    across = place_ref[0]
    right = right_ref[0].reshape(depth, right_ref.shape[3])
    total = jnp.dot(left, right, preferred_element_type=jnp.float32).astype(out_ref.dtype)
    for b in range(blocks):
        e = (across + b) % blocks
        out_ref[0, (e % 2) ^ (across % 2), e // 2] = total[b * tokens : (b + 1) * tokens]


def product(place, left, right):
    blocks, tokens, depth = left.shape
    pieces, cores, half, width = right.shape
    tiles = pieces // 2
    grid_spec = pltpu.PrefetchScalarGridSpec(
        num_scalar_prefetch=1,
        grid=(pieces,),
        in_specs=[
            pl.BlockSpec(memory_space=pltpu.VMEM),
            pl.BlockSpec(
                (1, cores, half, width), lambda z, place: (2 * (z % tiles) + (z // tiles + place[1]) % 2, 0, 0, 0)
            ),
        ],
        out_specs=pl.BlockSpec((1, 2, blocks // 2, tokens, width), lambda z, place: (z, 0, 0, 0, 0)),
    )
    return pl.pallas_call(
        product_kernel,
        grid_spec=grid_spec,
        out_shape=jax.ShapeDtypeStruct((pieces, 2, blocks // 2, tokens, width), jnp.bfloat16),
        compiler_params=pltpu.CompilerParams(vmem_limit_bytes=40 * 2**20),
        cost_estimate=pl.CostEstimate(
            flops=2 * blocks * tokens * right.size,
            bytes_accessed=2 * (left.size + right.size + pieces * blocks * tokens * width),
            transcendentals=0,
        ),
    )(place, left, right)


def solution(mesh):
    n_grp, n_kv, n_srv = mesh.shape["grp"], mesh.shape["kv"], mesh.shape["srv"]
    sy = n_srv // SX
    sizes = (n_grp, n_kv, SX, sy)
    fine = jax.sharding.Mesh(mesh.devices.reshape(sizes), ALL)

    def index(*place):
        total = 0
        for at, size in zip(place, sizes):
            total = total * size + at
        return total

    to_rows, to_owner = [[] for _ in range(SX)], [[], []]
    for c in range(n_grp):
        for x in range(SX):
            for b in range(SX):
                e = (x + b) % SX
                to_rows[b].append(((e // 2) * SX + 2 * c + e % 2, c * SX + x))
            for z in range(n_kv):
                for y in range(sy):
                    for h in range(2):
                        owner = index(x // 2, z, 2 * c + (x % 2 ^ h), y)
                        to_owner[h].append((index(c, z, x, y), owner))

    groups = [
        [index(c, z, 2 * a + (y + odd) % 2, y) for y in range(sy) for c in range(n_grp)]
        for z in range(n_kv)
        for a in range(SX // 2)
        for odd in range(2)
    ]

    def on_device(queries, keys, values, lengths, weight):
        tokens = queries.shape[0]
        core = lax.axis_index("grp")
        across = lax.axis_index("sx")
        shard = across * sy + lax.axis_index("sy")
        columns = lax.all_gather(weight[0], ALL, axis=0, tiled=True, axis_index_groups=groups)
        columns = columns.reshape(sy, n_grp, weight.shape[1], weight.shape[2])

        half = tokens // n_grp
        stacked = jnp.stack([keys[:, 0], values[:, 0]])
        mine = jnp.concatenate([fetch_behind(stacked, 1, n_srv), fetch_behind(stacked, 2, n_srv)], axis=1)
        own = lax.dynamic_slice_in_dim(queries[:, 0], core * half, half, 0)
        other = lax.dynamic_slice_in_dim(queries[:, 0], (1 - core) * half, half, 0)
        other = lax.ppermute(other, "grp", [(0, 1), (1, 0)])
        window = jnp.concatenate([mine, lax.ppermute(mine, "grp", [(0, 1), (1, 0)]), stacked], axis=1)
        behind = jnp.stack([1 + 2 * core, 2 + 2 * core, 3 - 2 * core, 4 - 2 * core, 0 * core])
        query_pos = shard * tokens + core * half + jnp.arange(half, dtype=jnp.int32)
        key_pos = ((shard - behind) * tokens)[:, None] + jnp.arange(tokens, dtype=jnp.int32)[None, :]
        first = core == 0
        both = jnp.concatenate([jnp.where(first, own, other), jnp.where(first, other, own)], axis=1)
        heads = attend(both, window[0], window[1], query_pos, key_pos.reshape(-1), lengths)
        along = jnp.stack([lax.ppermute(heads, ("grp", "sx"), to_rows[b]) for b in range(SX)])

        partial = product(jnp.stack([across, (across + lax.axis_index("sy")) % 2]), along, columns)
        width = partial.shape[4]
        summed = lax.psum_scatter(partial.reshape(n_kv, 2 * tokens, width), "kv", scatter_dimension=0)
        summed = summed.reshape(2, tokens, width)
        near, far = [lax.ppermute(summed[h], ALL, to_owner[h]) for h in range(2)]
        flip = (across + lax.axis_index("sy") + lax.axis_index("kv") // (n_kv // 2)) % 2 == 1
        return jnp.concatenate([jnp.where(flip, far, near), jnp.where(flip, near, far)], axis=1)

    q = P(("sx", "sy"), "kv", "grp")
    k = P(("sx", "sy"), "kv", None)
    placed = (q, k, k, P(), P("kv", "grp", ("sx", "sy")))
    return jax.shard_map(
        on_device, mesh=fine, in_specs=placed, out_specs=P(("sx", "sy"), ("grp", "kv")), check_vma=False
    )
```

```python
import math

import jax
import jax.numpy as jnp
from jax import lax
from jax.experimental import pallas as pl
from jax.experimental.pallas import tpu as pltpu
from jax.sharding import PartitionSpec as P

REACH = 4
ALL = ("grp", "kv", "sx", "sy")
SX = 4


def doc_starts(lengths, position):
    count = lengths.shape[0]
    before = jnp.arange(count)[None, :] < jnp.arange(count)[:, None]
    starts = jnp.sum(jnp.where(before, lengths[None, :], 0), axis=1)
    chosen = jnp.where(starts[None, :] <= position[:, None], starts[None, :], 0)
    return jnp.max(chosen, axis=1)


def attend(queries, window_keys, window_values, query_pos, key_pos, lengths):
    token_count = queries.shape[0]
    head_size = window_keys.shape[1]
    heads = queries.shape[1] // head_size
    split = queries.reshape(token_count, heads, head_size)
    scores = jnp.einsum("thd,wd->htw", split, window_keys, preferred_element_type=jnp.float32)
    scores = scores * (1.0 / math.sqrt(head_size))
    first_key = doc_starts(lengths, query_pos)
    allowed = (key_pos[None, :] >= first_key[:, None]) & (key_pos[None, :] <= query_pos[:, None])
    scores = jnp.where(allowed[None], scores, -jnp.inf)
    peak = jnp.max(scores, axis=2, keepdims=True)
    weights = jnp.exp(scores - peak)
    total = jnp.sum(weights, axis=2)
    numer = jnp.einsum(
        "htw,wd->thd", weights.astype(jnp.bfloat16), window_values, preferred_element_type=jnp.float32
    )
    result = numer / jnp.transpose(total, (1, 0))[..., None]
    return result.astype(jnp.bfloat16).reshape(token_count, heads * head_size)


def fetch_behind(stacked, near, n_srv):
    route = []
    for c in range(2):
        distance = near + 2 * c
        route += [(c * n_srv + i - distance, c * n_srv + i) for i in range(distance, n_srv)]
    return lax.ppermute(stacked, ("grp", "sx", "sy"), route)


def product_kernel(place_ref, left_ref, right_ref, out_ref):
    blocks, tokens, depth = left_ref.shape
    left = left_ref[...].reshape(blocks * tokens, depth)
    core = place_ref[0]
    pieces, _, _, width = right_ref.shape
    for piece in range(pieces):
        total = jnp.dot(
            left, right_ref[piece].reshape(depth, width), preferred_element_type=jnp.float32
        ).astype(out_ref.dtype)
        for x in range(blocks):
            out_ref[x // 2, (x % 2) ^ core, :, piece * width : (piece + 1) * width] = total[
                x * tokens : (x + 1) * tokens
            ]


def product(place, left, right):
    blocks, tokens, depth = left.shape
    pieces, cores, half, width = right.shape
    tiles = pieces // 2
    grid_spec = pltpu.PrefetchScalarGridSpec(
        num_scalar_prefetch=1,
        grid=(tiles,),
        in_specs=[
            pl.BlockSpec(memory_space=pltpu.VMEM),
            pl.BlockSpec((2, cores, half, width), lambda j, place: (j, 0, 0, 0)),
        ],
        out_specs=pl.BlockSpec(
            (blocks // 2, 2, tokens, 2 * width), lambda j, place: ((j + place[1]) % tiles, 0, 0, 0)
        ),
    )
    return pl.pallas_call(
        product_kernel,
        grid_spec=grid_spec,
        out_shape=jax.ShapeDtypeStruct((tiles * blocks // 2, 2, tokens, 2 * width), jnp.bfloat16),
        compiler_params=pltpu.CompilerParams(vmem_limit_bytes=56 * 2**20),
        cost_estimate=pl.CostEstimate(
            flops=2 * blocks * tokens * right.size,
            bytes_accessed=2 * (left.size + right.size + tiles * blocks * tokens * 2 * width),
            transcendentals=0,
        ),
    )(place, left, right)


def solution(mesh):
    n_grp, n_kv, n_srv = mesh.shape["grp"], mesh.shape["kv"], mesh.shape["srv"]
    sy = n_srv // SX
    sizes = (n_grp, n_kv, SX, sy)
    fine = jax.sharding.Mesh(mesh.devices.reshape(sizes), ALL)
    tiles = n_grp * n_kv // SX

    def index(*place):
        total = 0
        for at, size in zip(place, sizes):
            total = total * size + at
        return total

    def shift_of(x):
        return tiles - 1 + (x % 2) * (tiles // 2)

    to_rows, to_owner = [[] for _ in range(SX)], []
    for c in range(n_grp):
        for x in range(SX):
            for b in range(SX):
                to_rows[b].append(((c ^ (b % 2)) * SX + (x + c + 2 * (b // 2)) % SX, c * SX + x))
            for z in range(n_kv):
                owner = x * tiles + (z // 2 - shift_of(x)) % tiles
                to_x = (x + c + 2 * (z % 2)) % SX
                for y in range(sy):
                    to_owner.append((index(c, z, x, y), index(owner // n_kv, owner % n_kv, to_x, y)))

    def on_device(queries, keys, values, lengths, weight):
        tokens = queries.shape[0]
        core = lax.axis_index("grp")
        across = lax.axis_index("sx")
        shard = across * sy + lax.axis_index("sy")
        columns = lax.all_gather(weight[0], ("sy", "grp"), axis=0, tiled=True)
        columns = columns.reshape(sy, n_grp, weight.shape[1], weight.shape[2])

        half = tokens // n_grp
        stacked = jnp.stack([keys[:, 0], values[:, 0]])
        mine = jnp.concatenate([fetch_behind(stacked, 1, n_srv), fetch_behind(stacked, 2, n_srv)], axis=1)
        own = lax.dynamic_slice_in_dim(queries[:, 0], core * half, half, 0)
        other = lax.dynamic_slice_in_dim(queries[:, 0], (1 - core) * half, half, 0)
        other = lax.ppermute(other, "grp", [(0, 1), (1, 0)])
        window = jnp.concatenate([mine, lax.ppermute(mine, "grp", [(0, 1), (1, 0)]), stacked], axis=1)
        behind = jnp.stack([1 + 2 * core, 2 + 2 * core, 3 - 2 * core, 4 - 2 * core, 0 * core])
        query_pos = shard * tokens + core * half + jnp.arange(half, dtype=jnp.int32)
        key_pos = ((shard - behind) * tokens)[:, None] + jnp.arange(tokens, dtype=jnp.int32)[None, :]
        first = core == 0
        both = jnp.concatenate([jnp.where(first, own, other), jnp.where(first, other, own)], axis=1)
        heads = attend(both, window[0], window[1], query_pos, key_pos.reshape(-1), lengths)
        along = jnp.stack([lax.ppermute(heads, ("grp", "sx"), to_rows[b]) for b in range(SX)])

        partial = product(jnp.stack([core, shift_of(across)]), along, columns)
        partial = partial.reshape(n_kv, 2 * half, partial.shape[3])
        tile = lax.psum_scatter(partial, "kv", scatter_dimension=0)
        return lax.ppermute(tile, ALL, to_owner)

    q = P(("sx", "sy"), "kv", "grp")
    k = P(("sx", "sy"), "kv", None)
    placed = (q, k, k, P(), P("kv", "grp", ("sx", "sy")))
    return jax.shard_map(
        on_device, mesh=fine, in_specs=placed, out_specs=P(("sx", "sy"), ("grp", "kv")), check_vma=False
    )
```
